512 devices in a mesh: band: 32 (over z_hi, y, core), frame: 16 (over x, z_lo).
Axes of the slice: x: 4, y: 8, z: 8 (z_hi: 2, z_lo: 4; z = z_hi * 4 + z_lo), core: 2. Of those that a mesh axis runs over, the one named last changes fastest.
Arguments:
- hidden: bfloat16 [32, 16, 256, 1152], P('band', 'frame'), may hold values from -6 to 6
- timesteps: int32 [32, 16], P('band', 'frame'), may hold values from 0 to 29
- ada_table: float32 [30, 3, 1152], replicated, may hold values from -3 to 3
- w_qkv: bfloat16 [1152, 3456], P('frame'), may hold values from -0.1875 to 0.1875
- w_out: bfloat16 [1152, 1152], P('frame'), may hold values from -0.1875 to 0.1875
- q_gain: float32 [72], replicated, may hold values from 0.5 to 2
- k_gain: float32 [72], replicated, may hold values from 0.5 to 2
- fresh: bfloat16 [256, 1152], replicated, may hold values from -6 to 6
Outputs:
- queue_next: bfloat16 [32, 16, 256, 1152], P('band', 'frame')
The draws below stay inside these ranges and needn't reach their ends.
All inputs are finite; a program needn't handle non-finite values.
Results may differ from the reference program's by a relative error of at most 0.0095.
Values may be sent and summed in bfloat16 or wider, within the bound.
A program may use at most 64 MiB of HBM per device.

```python
import math
import jax
import jax.numpy as jnp
from jax import lax

D = 1152
HEADS = 16
HEAD_DIM = 72
TOK_DEV = 256
STEPS = 30
N_BAND = 32
N_FRAME = 16


def place_ends(array, rng, low, largest):
    dims = array.shape
    index_at = [jax.random.randint(jax.random.fold_in(rng, axis), (), 0, dims[axis]) for axis in range(len(dims))]
    array = array.at[tuple(index_at)].set(low)
    longest = dims.index(max(dims))
    index_at[longest] = (index_at[longest] + 1) % dims[longest]
    return array.at[tuple(index_at)].set(largest)


def shard_levels(rng, dims, shards, smallest, largest):
    def one(position, parts):
        heights = jax.random.uniform(jax.random.fold_in(jax.random.fold_in(rng, 6), position), (parts,), jnp.float32, smallest / len(shards), largest / len(shards))
        return jnp.repeat(jnp.exp(heights), dims[position] // parts).reshape((-1,) + (1,) * (len(dims) - position - 1))

    level = one(*shards[0])
    for cut in shards[1:]:
        level = level * one(*cut)
    return level


def scatter_about(rng, dims, spread, limit, cuts=(), kind=jnp.bfloat16):
    entries = spread * jax.random.normal(rng, dims, jnp.float32)
    if cuts:
        entries = entries * shard_levels(rng, dims, cuts, -0.22, 0.18)
    return jnp.clip(entries, -limit, limit).astype(kind)


def setup_inputs(seed: int = 0) -> dict:
    streams_of = jax.random.split(jax.random.key(seed), 9)
    hidden = scatter_about(streams_of[0], (N_BAND, N_FRAME, TOK_DEV, D), 1.0, 6.0, ((0, 32), (1, 16)))
    timesteps = place_ends(jax.random.randint(streams_of[1], (N_BAND, N_FRAME), 0, STEPS), jax.random.fold_in(streams_of[1], 1), 0, STEPS - 1).astype(jnp.int32)
    ada_table = scatter_about(streams_of[2], (STEPS, 3, D), 0.5, 3.0, (), jnp.float32)
    w_qkv = scatter_about(streams_of[3], (D, 3 * D), D ** -0.5, 0.1875, ((0, 16),))
    w_out = scatter_about(streams_of[4], (D, D), D ** -0.5, 0.1875, ((0, 16),))
    q_gain = jnp.clip(jnp.exp(jax.random.uniform(streams_of[5], (HEAD_DIM,), jnp.float32, math.log(0.5), math.log(2.0))), 0.5, 2.0)
    k_gain = jnp.clip(jnp.exp(jax.random.uniform(streams_of[6], (HEAD_DIM,), jnp.float32, math.log(0.5), math.log(2.0))), 0.5, 2.0)
    fresh = scatter_about(streams_of[7], (TOK_DEV, D), 1.0, 6.0)
    return dict(hidden=hidden, timesteps=timesteps, ada_table=ada_table, w_qkv=w_qkv, w_out=w_out, q_gain=q_gain, k_gain=k_gain, fresh=fresh)


def qk_norm(vec, gain):
    return vec * lax.rsqrt(lax.optimization_barrier(jnp.mean(vec * vec, axis=-1, keepdims=True)) + 1e-06) * gain

def rotate(vec, angle):
    half = vec.shape[-1] // 2
    first = vec[..., :half]
    second = vec[..., half:]
    cosine = jnp.cos(angle)
    sine = jnp.sin(angle)
    return jnp.concatenate([first * cosine - second * sine, first * sine + second * cosine], axis=-1)

def band_step(xb, tb, ada_table, w_qkv, w_out, q_gain, k_gain):
    nframe = xb.shape[0]
    rows = xb.shape[1]
    width = xb.shape[2]
    heads = HEADS
    head_dim = width // heads
    modul = ada_table[tb]
    shift = modul[:, 0][:, None, :]
    scale = modul[:, 1][:, None, :]
    gate = modul[:, 2][:, None, :]
    xf = xb.astype(jnp.float32)
    mean = lax.optimization_barrier(jnp.mean(xf, axis=-1, keepdims=True))
    centred = xf - mean
    var = lax.optimization_barrier(jnp.mean(centred * centred, axis=-1, keepdims=True))
    normed = (centred * lax.rsqrt(var + 1e-06) * (1.0 + scale) + shift).astype(jnp.bfloat16)
    qkv = jnp.dot(normed.reshape(nframe * rows, width), w_qkv, preferred_element_type=jnp.float32)
    qkv = qkv.reshape(nframe, rows, 3, heads, head_dim)
    half = head_dim // 2
    freq = jnp.power(10000.0, -2.0 * jnp.arange(half, dtype=jnp.float32) / head_dim)
    angle = jnp.arange(nframe, dtype=jnp.float32)[:, None, None, None] * freq
    query = rotate(qk_norm(qkv[:, :, 0], q_gain), angle).astype(jnp.bfloat16)
    keys = rotate(qk_norm(qkv[:, :, 1], k_gain), angle).astype(jnp.bfloat16)
    values = qkv[:, :, 2].astype(jnp.bfloat16)
    scores = jnp.einsum('fnhd,gnhd->nhfg', query.astype(jnp.float32), keys.astype(jnp.float32)) / jnp.sqrt(jnp.float32(head_dim))
    weights = jax.nn.softmax(scores, axis=-1).astype(jnp.bfloat16)
    attended = jnp.einsum('nhfg,gnhd->fnhd', weights.astype(jnp.float32), values.astype(jnp.float32)).astype(jnp.bfloat16)
    delta = jnp.dot(attended.reshape(nframe * rows, width), w_out, preferred_element_type=jnp.float32)
    delta = delta.reshape(nframe, rows, width)
    return (xf + gate * delta).astype(jnp.bfloat16)

def reference(hidden, timesteps, ada_table, w_qkv, w_out, q_gain, k_gain, fresh):

    def one_band(pair):
        return band_step(pair[0], pair[1], ada_table, w_qkv, w_out, q_gain, k_gain)
    updated = lax.map(one_band, (hidden, timesteps))
    nband, nframe, rows, width = hidden.shape
    flat = updated.reshape(nband * nframe, rows, width)
    moved = jnp.concatenate([fresh[None].astype(jnp.bfloat16), flat[:-1]], axis=0)
    return moved.reshape(nband, nframe, rows, width)
```

```python
import functools
import math

import jax
import jax.numpy as jnp
import numpy as np
from jax import lax
from jax.experimental import pallas as pl
from jax.experimental.pallas import tpu as pltpu
from jax.sharding import PartitionSpec as P

MESH = pl.DeviceIdType.MESH
D, HEADS, HD, ROWS, NF, STEPS, NB = 1152, 16, 72, 256, 16, 30, 32
TOK = ROWS // NF
F32, BF16 = jnp.float32, jnp.bfloat16
KMAIN, KREM = 1024, 256
KALL = 2 * KMAIN + 2 * KREM
V0, LO0, HI0 = KMAIN, 2 * KMAIN, 2 * KMAIN + KREM
OFFS = (0, -1, 1, 2)


def constants():
    source = np.full((KALL,), -1, np.int64)
    for c in range(2):
        for s in range(16):
            for r in range(32):
                source[c * 512 + s * 32 + r] = s * HD + c * 32 + r
    for m in range(2):
        for c in range(2):
            for s in range(16):
                for r in range(16):
                    source[V0 + (m * 2 + c) * 256 + s * 16 + r] = s * HD + c * 32 + m * 16 + r
    for s in range(16):
        for j in range(8):
            source[LO0 + s * 16 + j] = s * HD + 64 + j
            source[HI0 + s * 16 + 8 + j] = s * HD + 64 + j
    perm = np.zeros((D, KALL), np.float32)
    for n in range(KALL):
        if source[n] >= 0:
            perm[source[n], n] = 1.0
    lane = np.arange(D)
    gather = (lane[:, None] // HD == np.arange(128)[None, :]).astype(np.float32)
    spread = gather.T.copy()
    tile = (lane[None, :] % HD == np.arange(HD)[:, None]).astype(np.float32)
    half = HD // 2
    freq = np.power(10000.0, -2.0 * np.arange(half) / HD).astype(np.float32)
    angle = (np.arange(NF, dtype=np.float32)[:, None] * freq[None, :]).astype(np.float64)
    index = (lane % HD) % half
    first = (lane % HD) < half
    cosine = np.cos(angle)[:, index]
    sine = np.sin(angle)[:, index]
    rope = np.stack([cosine, np.where(first, -sine, 0.0), np.where(first, 0.0, sine)])
    rope = np.repeat(rope, 8, axis=1).astype(np.float32)
    masks = np.zeros((2, 4, 128, 384), np.float32)
    for g in range(2):
        for a in range(4):
            masks[g, a, :, 32 * a : 32 * a + 32] = 1.0
            masks[g, a, :, 128 + 32 * a : 128 + 32 * a + 32] = 1.0
            masks[g, a, :, 256 + 64 * g + 16 * a : 256 + 64 * g + 16 * a + 16] = 1.0
    masks = masks.reshape(2, 512, 384)
    return (
        jnp.asarray(perm, BF16),
        jnp.asarray(gather, BF16),
        jnp.asarray(spread, BF16),
        jnp.asarray(tile, F32),
        jnp.asarray(rope, F32),
        jnp.asarray(masks, BF16),
    )


def dot(a, b, **kw):
    return jnp.dot(a, b, preferred_element_type=F32, **kw)


def kernel(
    hidden, steps, table, wqkv, wout, q_gain, k_gain, perm_h, gather_h, spread_h, tile_h, rope_h, masks_h,
    out,
    eo, oc, wq_v, wo_v, x_v, table_v, tab, onehot, perm, gather, spread, tile, rope, masks, gain_v,
    modul, normed, xp, qf, rf, qb, kb, vb, vp, attp, delta, upd,
    send, recv, local, hsend, hrecv, osend, orecv, fsend, frecv,
):
    band = lax.axis_index("band")
    frame = lax.axis_index("frame")
    c = lax.rem(band, 2)
    y = lax.rem(band // 2, 8)
    par = lax.rem(y, 2)
    z_lo = lax.rem(frame, 4)
    x = frame // 4
    z = (band // 16) * 4 + z_lo

    def device(dx, dy, dz, core):
        xx = lax.rem(x + dx + 4, 4)
        yy = lax.rem(y + dy + 8, 8)
        zz = lax.rem(z + dz + 8, 8)
        return ((zz // 4) * 16 + yy * 2 + core, xx * 4 + lax.rem(zz, 4))

    a_up, a_dn = device(1 - c, 0, c, c), device(c - 1, 0, -c, c)
    b_up, b_dn = device(c, 0, 1 - c, c), device(-c, 0, c - 1, c)
    y_up, y_dn = device(0, 1, 0, c), device(0, -1, 0, c)
    sib = device(0, 0, 0, 1 - c)

    def shard(i, j):
        xx = lax.rem(x + i * (1 - c) + j * c + 4, 4)
        zz = lax.rem(z_lo + i * c + j * (1 - c) + 4, 4)
        return xx * 4 + zz

    def fetch(src, dst, k):
        cp = pltpu.make_async_copy(src, dst, local.at[k])
        cp.start()
        return cp

    got_w = [fetch(wqkv, wq_v, 0), fetch(wout, wo_v, 1)]
    own = pl.ds(pl.multiple_of(frame * TOK, TOK), TOK)
    got_own = fetch(hidden.at[own], x_v.at[own], 2)
    got_tab = fetch(table, table_v, 3)
    got_rest = [
        fetch(a, b, 4 + k)
        for k, (a, b) in enumerate(
            ((perm_h, perm), (gather_h, gather), (spread_h, spread), (tile_h, tile), (rope_h, rope), (masks_h, masks), (q_gain, gain_v.at[0]), (k_gain, gain_v.at[1]))
        )
    ]

    barrier = pltpu.get_barrier_semaphore()

    def greet(d):
        pl.semaphore_signal(barrier, inc=1, device_id=d, device_id_type=MESH)

    for d in (a_up, a_dn, b_up, b_dn, y_up, y_dn, sib):
        greet(d)
    for k in range(1, NF):
        greet((band, lax.rem(frame + k, NF)))

    @pl.when(jnp.logical_and(frame == 0, band > 0))
    def _():
        for k in range(NF):
            greet((band - 1, k))

    for cp in got_w:
        cp.wait()
    me = shard(0, 0)
    rest = wq_v[64:72, :].astype(F32)
    rest_o = wo_v[64:72, :].astype(F32)
    tails = (
        jnp.concatenate([rest[:, 0:D], rest[:, D : 2 * D]], axis=0).astype(BF16),
        jnp.concatenate([rest[:, 2 * D :], rest_o], axis=0).astype(BF16),
    )
    for cc in range(2):
        for m in range(2):
            eo[m, cc, me, 0:32, :] = wq_v[32 * cc : 32 * cc + 32, m * D : (m + 1) * D]
            eo[m, cc, me, 32:48, :] = wq_v[32 * cc + 16 * m : 32 * cc + 16 * m + 16, 2 * D :]
            eo[m, cc, me, 48:64, :] = tails[cc]
        oc[cc, me] = wo_v[32 * cc : 32 * cc + 32, :]

    pl.semaphore_wait(barrier, 22 + lax.min(NB - 1 - band, 1))

    pending = []

    def push(src, dst, d, rsem):
        k = len(pending)
        cp = pltpu.make_async_remote_copy(src, dst, send.at[k], recv.at[rsem], device_id=d, device_id_type=MESH)
        cp.start()
        pending.append(cp)

    def block(cls, i, j):
        if cls == "E":
            return eo.at[par, c, shard(i, j)]
        return oc.at[c, shard(i, j)]

    base = {"E": 0, "C": 16, "Y": 32, "SE": 48, "SC": 64, "SY": 80}

    def slot(kind, i, j):
        return base[kind] + (i + 1) * 4 + (j + 1)

    def push_block(cls, i, j, d, ri, rj):
        ref = block(cls, i, j)
        push(ref, ref, d, slot(cls, ri, rj))

    def expect(ref, rsem):
        pltpu.make_async_remote_copy(ref, ref, send.at[0], recv.at[rsem], device_id=sib, device_id_type=MESH).wait_recv()

    def start_own(cls):
        push_block(cls, 0, 0, b_up, 0, -1)
        push_block(cls, 0, 0, b_dn, 0, 1)
        push_block(cls, 0, 0, a_up, -1, 0)
        push_block(cls, 0, 0, a_dn, 1, 0)

    turn = [0]
    y_route = {}

    def take(cls, i, j):
        expect(block(cls, i, j), slot(cls, i, j))
        if j == 0:
            if cls == "E" and i == -1:
                push_block(cls, i, j, a_up, 2, 0)
            if cls == "C" and i == 1:
                push_block(cls, i, j, a_dn, 2, 0)
            push_block(cls, i, j, b_up, i, -1)
            push_block(cls, i, j, b_dn, i, 1)
        elif j == -1 and i in (0, -1):
            push_block(cls, i, j, b_up, i, 2)
        elif j == 1 and i in (1, 2):
            push_block(cls, i, j, b_dn, i, 2)
        ref = block(cls, i, j)
        if cls == "E":
            ycols = eo.at[par, c, shard(i, j), pl.ds(0, 48)]
            up = turn[0] % 2 == 0
            turn[0] += 1
            push(ycols, ycols, y_up if up else y_dn, slot("Y", i, j))
            y_route[(i, j)] = up
        push(ref, ref, sib, slot("S" + cls, i, j))

    def take_y(i, j):
        ref = eo.at[1 - par, c, shard(i, j), pl.ds(0, 48)]
        expect(ref, slot("Y", i, j))
        push(ref, ref, sib, slot("SY", i, j))

    ORDER = (
        (-1, 0), (1, 0), (0, -1), (0, 1), (2, 0),
        (-1, -1), (-1, 1), (1, 1), (1, -1), (2, 1), (2, -1),
        (0, 2), (-1, 2), (1, 2), (2, 2),
    )

    start_own("E")

    step = steps[0, 0]
    lanes = lax.broadcasted_iota(jnp.int32, (8, 128), 1)
    onehot[frame] = (lanes == step).astype(F32)
    h_copies = []
    for k in range(1, NF):
        to = lax.rem(frame + k, NF)
        rows = pl.ds(pl.multiple_of(to * TOK, TOK), TOK)
        h = pltpu.make_async_remote_copy(hidden.at[rows], x_v.at[own], hsend.at[k], hrecv.at[k], device_id=(band, to), device_id_type=MESH)
        o = pltpu.make_async_remote_copy(onehot.at[frame], onehot.at[frame], osend.at[k], orecv.at[k], device_id=(band, to), device_id_type=MESH)
        h.start()
        o.start()
        h_copies += [h, o]
    start_own("C")

    for i, j in ORDER[:5]:
        take("E", i, j)

    got_tab.wait()
    got_own.wait()
    for cp in got_rest:
        cp.wait()
    tab[...] = jnp.zeros_like(tab)
    for j in range(3):
        tab[j, 0:STEPS, :] = table_v[j]

    for i, j in ORDER[:5]:
        take("C", i, j)
    for i, j in ORDER[5:]:
        take("E", i, j)

    for k in range(1, NF):
        back = lax.rem(frame - k + NF, NF)
        rows = pl.ds(pl.multiple_of(back * TOK, TOK), TOK)
        pltpu.make_async_remote_copy(x_v.at[rows], x_v.at[rows], hsend.at[k], hrecv.at[k], device_id=sib, device_id_type=MESH).wait_recv()
        pltpu.make_async_remote_copy(onehot.at[back], onehot.at[back], osend.at[k], orecv.at[k], device_id=sib, device_id_type=MESH).wait_recv()

    oh = onehot[...].reshape(128, 128)
    for j in range(3):
        modul[j] = dot(oh, tab[j], precision=lax.Precision.HIGHEST)

    def norm_frame(f, _):
        r16 = pl.ds(pl.multiple_of(f * TOK, TOK), TOK)
        r8 = pl.multiple_of(f * 8, 8)
        v = x_v[r16, :].astype(F32)
        mean = jnp.mean(v, axis=-1, keepdims=True)
        cen = v - mean
        var = jnp.mean(cen * cen, axis=-1, keepdims=True)
        cen = cen * lax.rsqrt(var + 1e-06)
        scale = 1.0 + modul[1, pl.ds(r8, 8), :]
        shift = modul[0, pl.ds(r8, 8), :]
        normed[pl.ds(r8, 8), :] = cen[0:8] * scale + shift
        normed[pl.ds(pl.multiple_of(r8 + 128, 8), 8), :] = cen[8:16] * scale + shift
        return 0

    lax.fori_loop(0, NF, norm_frame, 0, unroll=4)
    qb[...] = normed[...].astype(BF16)

    def permute(n, _):
        cols = pl.ds(pl.multiple_of(n * 512, 512), 512)
        xp[:, cols] = dot(qb[...], perm[:, cols]).astype(BF16)
        return 0

    lax.fori_loop(0, KALL // 512, permute, 0)

    for i, j in ORDER[5:]:
        take("C", i, j)
    for i, j in ORDER:
        take_y(i, j)
    for i, j in ORDER:
        ref = eo.at[par, 1 - c, shard(i, j)]
        expect(ref, slot("SE", i, j))
    for i, j in ORDER:
        ref = eo.at[1 - par, 1 - c, shard(i, j), pl.ds(0, 48)]
        expect(ref, slot("SY", i, j))

    NT = 384

    def project(dst, pieces):
        def one(n, _):
            cols = pl.ds(pl.multiple_of(n * NT, NT), NT)
            total = None
            for lhs, rhs in pieces:
                term = dot(lhs(), rhs(cols))
                total = term if total is None else total + term
            dst[:, cols] = total.astype(dst.dtype)
            return 0

        lax.fori_loop(0, D // NT, one, 0)

    def lhs_at(ref, start, width):
        return lambda: ref[:, start : start + width]

    def rhs_at(m, cc, lo, n):
        return lambda cols: eo[m, cc, :, lo : lo + n, cols].reshape(16 * n, NT)

    def heads_of(m, dst):
        project(qf, [
            (lhs_at(xp, 0, 512), rhs_at(m, 0, 0, 32)),
            (lhs_at(xp, 512, 512), rhs_at(m, 1, 0, 32)),
            (lhs_at(xp, LO0 if m == 0 else HI0, KREM), rhs_at(par, 0, 48, 16)),
        ])
        squares = qf[...]
        ss = dot((squares * squares).astype(BF16), gather[...])
        r = lax.rsqrt(ss * (1.0 / HD) + 1e-06)
        hi = r.astype(BF16)
        lo = (r - hi.astype(F32)).astype(BF16)
        rf[...] = dot(hi, spread[...]) + dot(lo, spread[...])
        gain = dot(jnp.broadcast_to(gain_v[m], (8, HD)), tile[...], precision=lax.Precision.HIGHEST)[0:1, :]

        def turn_rows(g, _):
            r32 = pl.ds(pl.multiple_of(g * 32, 32), 32)
            t32 = pl.ds(pl.multiple_of(lax.rem(g, 4) * 32, 32), 32)
            v = qf[r32, :] * rf[r32, :] * gain
            w = v * rope[0, t32, :]
            w = w + pltpu.roll(v, D - HD // 2, 1) * rope[1, t32, :]
            w = w + pltpu.roll(v, HD // 2, 1) * rope[2, t32, :]
            dst[r32, :] = w.astype(BF16)
            return 0

        lax.fori_loop(0, ROWS // 32, turn_rows, 0)

    heads_of(0, qb)
    heads_of(1, kb)
    project(vb, [
        (lhs_at(xp, V0 + (m * 2 + cc) * 256, 256), rhs_at(m, cc, 32, 16)) for m in range(2) for cc in range(2)
    ] + [(lhs_at(xp, LO0, KREM), rhs_at(par, 1, 48, 16))])
    vp[:, 0:512] = dot(vb[...], perm[:, 0:512]).astype(BF16)
    vp[:, 512:1024] = dot(vb[...], perm[:, 512:1024]).astype(BF16)
    vp[:, 1024:1280] = dot(vb[...], perm[:, HI0:KALL]).astype(BF16)

    same = (
        lax.rem(lax.broadcasted_iota(jnp.int32, (128, 128), 0), 8)
        == lax.rem(lax.broadcasted_iota(jnp.int32, (128, 128), 1), 8)
    ).astype(F32)
    factor = 1.0 / math.sqrt(HD)

    def attend(h, _):
        rows = pl.ds(pl.multiple_of(h * 128, 128), 128)
        num_rem = den_rem = None
        for g in range(4):
            probs = []
            for a in range(4):
                hd = 4 * g + a
                w = (HD * hd) // 128 * 128
                width = min(256, D - w)
                lane = lax.broadcasted_iota(jnp.int32, (16, width), 1) + w
                pick = jnp.logical_and(lane >= HD * hd, lane < HD * (hd + 1)).astype(F32).astype(BF16)
                pick = jnp.concatenate([pick] * 8, axis=0)
                kw = kb[rows, w : w + width] * pick
                sc = lax.dot_general(qb[rows, w : w + width], kw, (((1,), (1,)), ((), ())), preferred_element_type=F32)
                probs.append((jnp.exp(sc * factor) * same).astype(BF16))
            p4 = jnp.concatenate(probs, axis=1)
            vg = jnp.concatenate([
                vp[rows, g * 128 : g * 128 + 128],
                vp[rows, 512 + g * 128 : 512 + g * 128 + 128],
                vp[rows, 1024 + (g // 2) * 128 : 1024 + (g // 2) * 128 + 128],
            ], axis=1)
            mk = masks[g % 2]
            num = dot(p4, jnp.concatenate([vg] * 4, axis=0) * mk)
            den = dot(p4, mk)
            inv = 1.0 / den[:, 0:128]
            attp[rows, g * 128 : g * 128 + 128] = (num[:, 0:128] * inv).astype(BF16)
            attp[rows, 512 + g * 128 : 512 + g * 128 + 128] = (num[:, 128:256] * inv).astype(BF16)
            if g % 2 == 0:
                num_rem, den_rem = num[:, 256:384], den[:, 256:384]
            else:
                lo = 1024 + (g // 2) * 128
                attp[rows, lo : lo + 128] = ((num_rem + num[:, 256:384]) / (den_rem + den[:, 256:384])).astype(BF16)
        return 0

    lax.fori_loop(0, 2, attend, 0)

    for i, j in ORDER:
        expect(oc.at[1 - c, shard(i, j)], slot("SC", i, j))

    project(delta, [
        (lhs_at(attp, 0, 512), lambda cols: oc[0, :, :, cols].reshape(512, NT)),
        (lhs_at(attp, 512, 512), lambda cols: oc[1, :, :, cols].reshape(512, NT)),
        (lhs_at(attp, 1024, KREM), rhs_at(par, 1, 48, 16)),
    ])

    f_copies = []
    for k in range(NF):
        f = lax.rem(frame + k, NF)
        r16 = pl.ds(pl.multiple_of(f * TOK, TOK), TOK)
        r8 = pl.multiple_of(f * 8, 8)
        gate = modul[2, pl.ds(r8, 8), :]
        both = jnp.concatenate([
            gate * delta[pl.ds(r8, 8), :],
            gate * delta[pl.ds(pl.multiple_of(r8 + 128, 8), 8), :],
        ], axis=0)
        upd[r16, :] = (x_v[r16, :].astype(F32) + both).astype(BF16)
        last = f // (NF - 1)
        to_band = band + last
        to_frame = lax.rem(f + 1, NF)
        cp = pltpu.make_async_remote_copy(upd.at[r16], out.at[own], fsend.at[k], frecv.at[frame], device_id=(to_band, to_frame), device_id_type=MESH)
        here = jnp.logical_and(to_band == band, to_frame == frame)
        inside = to_band < NB
        if k < NF - 1:
            pl.when(inside)(cp.start)
            f_copies.append((inside, cp))
        else:
            away = jnp.logical_and(inside, frame == 0)
            pl.when(away)(cp.start)
            f_copies.append((away, cp))
            stay = pltpu.make_async_copy(upd.at[r16], out.at[own], local.at[0])

            @pl.when(frame > 0)
            def _():
                stay.start()
                stay.wait()

    def arrive(f):
        rows = pl.ds(pl.multiple_of(f * TOK, TOK), TOK)
        pltpu.make_async_remote_copy(out.at[rows], out.at[rows], fsend.at[0], frecv.at[f], device_id=sib, device_id_type=MESH).wait_recv()

    for f in range(NF):
        comes = jnp.logical_or(jnp.logical_and(frame > 0, frame != f), jnp.logical_and(frame == 0, band > 0))
        pl.when(comes)(functools.partial(arrive, f))

    for cond, cp in f_copies:
        pl.when(cond)(cp.wait_send)
    for cp in h_copies:
        cp.wait_send()
    for cp in pending:
        cp.wait_send()


def local_step(hidden, timesteps, ada_table, w_qkv, w_out, q_gain, k_gain, fresh):
    hbm = pl.BlockSpec(memory_space=pl.ANY)
    consts = constants()
    shapes = [
        pltpu.VMEM((2, 2, 16, 64, D), BF16),
        pltpu.VMEM((2, 16, 32, D), BF16),
        pltpu.VMEM((72, 3 * D), BF16),
        pltpu.VMEM((72, D), BF16),
        pltpu.VMEM((ROWS, D), BF16),
        pltpu.VMEM((3, STEPS, D), F32),
        pltpu.VMEM((3, 128, D), F32),
        pltpu.VMEM((NF, 8, 128), F32),
        *[pltpu.VMEM(a.shape, a.dtype) for a in consts],
        pltpu.VMEM((2, 1, HD), F32),
        pltpu.VMEM((3, 128, D), F32),
        pltpu.VMEM((ROWS, D), F32),
        pltpu.VMEM((ROWS, KALL), BF16),
        pltpu.VMEM((ROWS, D), F32),
        pltpu.VMEM((ROWS, D), F32),
        pltpu.VMEM((ROWS, D), BF16),
        pltpu.VMEM((ROWS, D), BF16),
        pltpu.VMEM((ROWS, D), BF16),
        pltpu.VMEM((ROWS, 1280), BF16),
        pltpu.VMEM((ROWS, 1280), BF16),
        pltpu.VMEM((ROWS, D), F32),
        pltpu.VMEM((ROWS, D), BF16),
        pltpu.SemaphoreType.DMA((96,)),
        pltpu.SemaphoreType.DMA((96,)),
        pltpu.SemaphoreType.DMA((12,)),
        *[pltpu.SemaphoreType.DMA((NF,)) for _ in range(6)],
    ]
    moved = pl.pallas_call(
        kernel,
        out_shape=jax.ShapeDtypeStruct((ROWS, D), BF16),
        in_specs=[hbm, pl.BlockSpec(memory_space=pltpu.SMEM)] + [hbm] * (5 + len(consts)),
        out_specs=hbm,
        scratch_shapes=shapes,
        compiler_params=pltpu.CompilerParams(collective_id=0, has_side_effects=True, vmem_limit_bytes=56 << 20),
        name="queue_step",
    )(hidden[0, 0], timesteps, jnp.transpose(ada_table, (1, 0, 2)), w_qkv, w_out, q_gain[None], k_gain[None], *consts)
    first = jnp.logical_and(lax.axis_index("band") == 0, lax.axis_index("frame") == 0)
    return jnp.where(first, fresh, moved)[None, None]


def solution(mesh):
    return jax.shard_map(
        local_step,
        mesh=mesh,
        in_specs=(
            P("band", "frame", None, None),
            P("band", "frame"),
            P(),
            P("frame", None),
            P("frame", None),
            P(),
            P(),
            P(),
        ),
        out_specs=P("band", "frame", None, None),
        check_vma=False,
    )
```

```python
import functools
import math

import jax
import jax.numpy as jnp
import numpy as np
from jax import lax
from jax.experimental import pallas as pl
from jax.experimental.pallas import tpu as pltpu
from jax.sharding import PartitionSpec as P

MESH = pl.DeviceIdType.MESH
D, HEADS, HD, ROWS, NF, STEPS, NB = 1152, 16, 72, 256, 16, 30, 32
TOK = ROWS // NF
F32, BF16 = jnp.float32, jnp.bfloat16
KMAIN, KREM = 1024, 256
LO0, HI0, O0 = KMAIN, KMAIN + KREM, KMAIN + 2 * KREM
KALL = O0 + KMAIN
KINDS = ("E", "F", "C", "YE", "YF", "YC")
WORK = ("tab", "mod", "rope", "ln", "p0", "p1", "p2", "f0", "f1", "f2", "g0", "g1", "g2", "v", "vp", "a0", "a1")
HOPS = (
    ((-1, 0), (1, 0), (0, -1), (0, 1)),
    ((2, 0), (-1, -1), (-1, 1), (1, 1), (1, -1), (0, 2)),
    ((2, 1), (2, -1), (-1, 2), (1, 2)),
    ((2, 2),),
)
SCHEDULE = (
    ("E", -1), (3, 0), ("F", -1), ("C", -1), ("E", 0, 1), ("tab", 0), ("mod", 0), ("rope", 0),
    ("F", 0), ("C", 0), ("E", 1, 1), ("F", 1), ("C", 1), ("E", 2, 1), ("YE", 0), ("F", 2),
    ("C", 2), ("E", 3), ("YE", 1), ("F", 3), ("ln", 0), ("YE", 2), ("p0", 0), ("YF", 0),
    ("YF", 1), ("YC", 0), ("p1", 0), ("YE", 3), ("p2", 0), ("C", 3), ("f0", 0), ("YF", 2),
    ("YF", 3), ("f1", 0), ("f2", 0), ("YC", 1), ("g0", 0), ("g1", 0), ("g2", 0), ("YC", 2),
    ("v", 0), ("YC", 3), ("vp", 0), ("a0", 0), ("a1", 0),
)


def constants():
    source = np.full((KALL,), -1, np.int64)
    for c in range(2):
        for s in range(16):
            for r in range(32):
                source[O0 + c * 512 + s * 32 + r] = s * HD + c * 32 + r
    for m in range(2):
        for c in range(2):
            for s in range(16):
                for r in range(16):
                    source[(m * 2 + c) * 256 + s * 16 + r] = s * HD + c * 32 + m * 16 + r
    for s in range(16):
        for j in range(8):
            source[LO0 + s * 16 + j] = s * HD + 64 + j
            source[HI0 + s * 16 + 8 + j] = s * HD + 64 + j
    perm = np.zeros((D, KALL), np.float32)
    for n in range(KALL):
        if source[n] >= 0:
            perm[source[n], n] = 1.0
    lane = np.arange(D)
    gather = (lane[:, None] // HD == np.arange(128)[None, :]).astype(np.float32)
    spread = gather.T.copy()
    tile = (lane[None, :] % HD == np.arange(HD)[:, None]).astype(np.float32)
    half = HD // 2
    freq = np.power(10000.0, -2.0 * np.arange(half) / HD).astype(np.float32)
    angle = (np.arange(NF, dtype=np.float32)[:, None] * freq[None, :]).astype(np.float64)
    index = (lane % HD) % half
    first = (lane % HD) < half
    cosine = np.cos(angle)[:, index]
    sine = np.sin(angle)[:, index]
    rope = np.stack([cosine, np.where(first, -sine, 0.0), np.where(first, 0.0, sine)])
    rope = np.repeat(rope, 8, axis=1).astype(np.float32)
    masks = np.zeros((2, 4, 128, 384), np.float32)
    for g in range(2):
        for a in range(4):
            masks[g, a, :, 32 * a : 32 * a + 32] = 1.0
            masks[g, a, :, 128 + 32 * a : 128 + 32 * a + 32] = 1.0
            masks[g, a, :, 256 + 64 * g + 16 * a : 256 + 64 * g + 16 * a + 16] = 1.0
    masks = masks.reshape(2, 512, 384)
    return (
        jnp.asarray(perm, BF16),
        jnp.asarray(gather, BF16),
        jnp.asarray(spread, BF16),
        jnp.asarray(tile, F32),
        jnp.asarray(rope, F32),
        jnp.asarray(masks, BF16),
    )


def dot(a, b, **kw):
    return jnp.dot(a, b, preferred_element_type=F32, **kw)


def kernel(
    hidden, steps, table, wqkv, wout, q_gain, k_gain, perm_h, gather_h, spread_h, tile_h, rope_h, masks_h,
    out,
    eo, oc, wq_v, wo_v, x_v, table_v, tab, onehot, perm, gather, spread, tile, rope, masks, gain_v,
    modul, turned, normed, nb, xp, qf, rf, qk, vb, vp, attp, delta, upd,
    send, recv, local,
):
    band = lax.axis_index("band")
    frame = lax.axis_index("frame")
    c = lax.rem(band, 2)
    y = lax.rem(band // 2, 8)
    par = lax.rem(y, 2)
    z_lo = lax.rem(frame, 4)
    x = frame // 4
    z = (band // 16) * 4 + z_lo

    def device(dx, dy, dz, core):
        xx = lax.rem(x + dx + 4, 4)
        yy = lax.rem(y + dy + 8, 8)
        zz = lax.rem(z + dz + 8, 8)
        return ((zz // 4) * 16 + yy * 2 + core, xx * 4 + lax.rem(zz, 4))

    y_up, y_dn = device(0, 1, 0, c), device(0, -1, 0, c)
    sib = device(0, 0, 0, 1 - c)

    def shard(ax, i, j):
        xx = lax.rem(x + i * ax + j * (1 - ax) + 4, 4)
        zz = lax.rem(z_lo + i * (1 - ax) + j * ax + 4, 4)
        return xx * 4 + zz

    def fetch(src, dst, k):
        cp = pltpu.make_async_copy(src, dst, local.at[k])
        cp.start()
        return cp

    got_w = [fetch(wqkv, wq_v, 0), fetch(wout, wo_v, 1)]
    own = pl.ds(pl.multiple_of(frame * TOK, TOK), TOK)
    got_own = fetch(hidden.at[own], x_v.at[own], 2)
    got_tab = fetch(table, table_v, 3)
    got_rest = [
        fetch(a, b, 4 + k)
        for k, (a, b) in enumerate(
            ((perm_h, perm), (gather_h, gather), (spread_h, spread), (tile_h, tile), (rope_h, rope), (masks_h, masks), (q_gain, gain_v.at[0]), (k_gain, gain_v.at[1]))
        )
    ]

    barrier = pltpu.get_barrier_semaphore()

    def greet(d):
        pl.semaphore_signal(barrier, inc=1, device_id=d, device_id_type=MESH)

    for move in ((1, 0, 0), (-1, 0, 0), (0, 1, 0), (0, -1, 0), (0, 0, 1), (0, 0, -1)):
        greet(device(*move, c))
    greet(sib)
    for k in range(1, NF):
        greet((band, lax.rem(frame + k, NF)))

    @pl.when(jnp.logical_and(frame == 0, band > 0))
    def _():
        for k in range(NF):
            greet((band - 1, k))

    for cp in got_w:
        cp.wait()
    me = frame
    rest = wq_v[64:72, :].astype(F32)
    rest_o = wo_v[64:72, :].astype(F32)
    tails = (
        jnp.concatenate([rest[:, 0:D], rest[:, D : 2 * D]], axis=0).astype(BF16),
        jnp.concatenate([rest[:, 2 * D :], rest_o], axis=0).astype(BF16),
    )
    for cc in range(2):
        for m in range(2):
            eo[m, cc, me, 0:32, :] = wq_v[32 * cc : 32 * cc + 32, m * D : (m + 1) * D]
            eo[m, cc, me, 32:48, :] = tails[cc]
            eo[m, cc, me, 48:64, :] = wq_v[32 * cc + 16 * m : 32 * cc + 16 * m + 16, 2 * D :]
            oc[m, cc, me] = wo_v[32 * cc + 16 * m : 32 * cc + 16 * m + 16, :]

    pl.semaphore_wait(barrier, 22 + lax.min(NB - 1 - band, 1))

    def push(src, dst, d, ssem, rsem):
        pltpu.make_async_remote_copy(src, dst, send.at[ssem], recv.at[rsem], device_id=d, device_id_type=MESH).start()

    def settle(ref, ssem=None, rsem=None):
        cp = pltpu.make_async_remote_copy(ref, ref, send.at[ssem or 0], recv.at[rsem or 0], device_id=sib, device_id_type=MESH)
        if rsem is None:
            cp.wait_send()
        else:
            cp.wait_recv()

    SPAN = {"E": (0, 48), "F": (48, 16), "YE": (0, 32), "YF": (48, 16), "C": (0, 16), "YC": (0, 16)}

    def block(kind, i, j):
        which = shard(FIRST_X[kind[-1]], i, j)
        m = 1 - par if kind[0] == "Y" else par
        if kind[-1] == "C":
            return oc.at[m, c, which]
        start, size = SPAN[kind]
        return eo.at[m, c, which, pl.ds(start, size)]

    def same_bytes(count, kind):
        return eo.at[0, 0, pl.ds(0, count), pl.ds(0, SPAN[kind][1])]

    def hop_of(i, j):
        return [n for n, hop in enumerate(HOPS) if (i, j) in hop][0]

    def slot(kind, i, j):
        if kind == "E":
            return 4 * i + j + 5
        return 16 + 4 * (KINDS.index(kind) - 1) + hop_of(i, j)

    SIB, HID, HOT, FIN = 36, 42, 43, 44

    def push_block(kind, i, j, d, ri, rj):
        ref = block(kind, i, j)
        push(ref, ref, d, KINDS.index(kind), slot(kind, ri, rj))

    FIRST_X = {"E": 1 - c, "F": 1 - c, "C": 0}

    def ways(kind):
        ax = FIRST_X[kind]
        return device(ax, 0, 1 - ax, c), device(-ax, 0, ax - 1, c), device(1 - ax, 0, ax, c), device(ax - 1, 0, -ax, c)

    WAYS = {kind: ways(kind) for kind in FIRST_X}

    def start_own(kind):
        a_up, a_dn, b_up, b_dn = WAYS[kind]
        push_block(kind, 0, 0, b_up, 0, -1)
        push_block(kind, 0, 0, b_dn, 0, 1)
        push_block(kind, 0, 0, a_up, -1, 0)
        push_block(kind, 0, 0, a_dn, 1, 0)

    turn = [0]

    def forward(kind, i, j):
        if kind[0] != "Y":
            a_up, a_dn, b_up, b_dn = WAYS[kind]
            if j == 0:
                if kind != "C" and i == -1:
                    push_block(kind, i, j, a_up, 2, 0)
                if kind == "C" and i == 1:
                    push_block(kind, i, j, a_dn, 2, 0)
                push_block(kind, i, j, b_up, i, -1)
                push_block(kind, i, j, b_dn, i, 1)
            elif j == -1 and i in (0, -1):
                push_block(kind, i, j, b_up, i, 2)
            elif j == 1 and i in (1, 2):
                push_block(kind, i, j, b_dn, i, 2)
            ref = block(kind, i, j)
            if kind == "E":
                ref = eo.at[par, c, shard(FIRST_X[kind], i, j), pl.ds(0, 32)]
            other = "Y" + kind
            push(ref, ref, y_up if turn[0] % 2 == 0 else y_dn, KINDS.index(other), slot(other, i, j))
            turn[0] += 1
        ref = block(kind, i, j)
        push(ref, ref, sib, 6 + KINDS.index(kind), SIB + KINDS.index(kind))

    def take(kind, hop, hidden_after):
        blocks = HOPS[hop]
        if kind != "E":
            settle(same_bytes(len(blocks), kind), rsem=slot(kind, *blocks[0]))
        for i, j in blocks:
            if kind == "E":
                settle(block(kind, i, j), rsem=slot(kind, i, j))
            forward(kind, i, j)
            send_hidden(hidden_after)

    def from_sibling(kinds):
        for kind in kinds:
            settle(same_bytes(NF - 1, kind), rsem=SIB + KINDS.index(kind))

    step = steps[0, 0]
    lanes = lax.broadcasted_iota(jnp.int32, (8, 128), 1)
    onehot[frame] = (lanes == step).astype(F32)
    def send_onehots():
        for k in range(1, NF):
            to = lax.rem(frame + k, NF)
            push(onehot.at[frame], onehot.at[frame], (band, to), 13, HOT)

    todo = [8, 7, 9, 6, 10, 5, 11, 4, 12, 3, 13, 2, 14, 1, 15]

    def send_hidden(count):
        for _ in range(min(count, len(todo))):
            to = lax.rem(frame + todo.pop(0), NF)
            rows = pl.ds(pl.multiple_of(to * TOK, TOK), TOK)
            push(hidden.at[rows], x_v.at[own], (band, to), 12, HID)

    NT = 384

    def project(dst, lhs, rhs):
        def one(n, _):
            cols = pl.ds(pl.multiple_of(n * NT, NT), NT)
            dst[:, cols] = dot(lhs(), jnp.concatenate([r(cols) for r in rhs], axis=0)).astype(dst.dtype)
            return 0

        lax.fori_loop(0, D // NT, one, 0)

    def piece(m, cc, lo):
        return lambda cols: eo[m, cc, :, lo : lo + 16, cols].reshape(256, NT)

    factor = math.log2(math.e) / math.sqrt(HD)

    def work_tab():
        got_tab.wait()
        tab[...] = jnp.zeros_like(tab)
        for j in range(3):
            tab[j, 0:STEPS, :] = table_v[j]

    def work_mod():
        settle(onehot.at[pl.ds(0, NF - 1)], rsem=HOT)
        oh = onehot[...].reshape(128, 128)
        for j in range(3):
            modul[j] = dot(oh, tab[j], precision=lax.Precision.HIGHEST)

    def work_rope():
        for cp in got_rest:
            cp.wait()
        for m in range(2):
            g = dot(jnp.broadcast_to(gain_v[m], (8, HD)), tile[...], precision=lax.Precision.HIGHEST)
            if m == 0:
                g = g * factor
            rolled = (g, pltpu.roll(g, D - HD // 2, 1), pltpu.roll(g, HD // 2, 1))
            for j in range(3):
                turned[m, j] = rope[j] * rolled[j][0:1, :]

    def norm_frame(f, _):
        r16 = pl.ds(pl.multiple_of(f * TOK, TOK), TOK)
        r8 = pl.multiple_of(f * 8, 8)
        v = x_v[r16, :].astype(F32)
        mean = jnp.mean(v, axis=-1, keepdims=True)
        cen = v - mean
        var = jnp.mean(cen * cen, axis=-1, keepdims=True)
        cen = cen * lax.rsqrt(var + 1e-06)
        scale = 1.0 + modul[1, pl.ds(r8, 8), :]
        shift = modul[0, pl.ds(r8, 8), :]
        normed[pl.ds(r8, 8), :] = cen[0:8] * scale + shift
        normed[pl.ds(pl.multiple_of(r8 + 128, 8), 8), :] = cen[8:16] * scale + shift
        return 0

    def work_ln():
        got_own.wait()
        settle(x_v.at[pl.ds(0, ROWS - TOK)], rsem=HID)
        lax.fori_loop(0, NF, norm_frame, 0, unroll=4)
        nb[...] = normed[...].astype(BF16)

    def work_permute(n):
        cols = pl.ds(n * 512, 512)
        xp[:, cols] = dot(nb[...], perm[:, cols]).astype(BF16)

    def work_multiply(m, kind):
        from_sibling((kind,))
        last = pl.ds(pl.multiple_of(LO0 + KREM * m, KREM), KREM)
        project(
            qf,
            lambda: jnp.concatenate([xp[:, 0:KMAIN], xp[:, last]], axis=1),
            [piece(m, cc, 16 * half) for half in range(2) for cc in range(2)] + [piece(par, 0, 32)],
        )

    def work_stats():
        squares = qf[...]
        ss = dot((squares * squares).astype(BF16), gather[...])
        r = lax.rsqrt(ss * (1.0 / HD) + 1e-06)
        hi = r.astype(BF16)
        lo = (r - hi.astype(F32)).astype(BF16)
        rf[...] = dot(jnp.concatenate([hi, lo], axis=1), jnp.concatenate([spread[...], spread[...]], axis=0))

    def work_turn(m):
        def turn_rows(g, _):
            r32 = pl.ds(pl.multiple_of(g * 32, 32), 32)
            t32 = pl.ds(pl.multiple_of(lax.rem(g, 4) * 32, 32), 32)
            v = qf[r32, :] * rf[r32, :]
            w = v * turned[m, 0, t32, :]
            w = w + pltpu.roll(v, D - HD // 2, 1) * turned[m, 1, t32, :]
            w = w + pltpu.roll(v, HD // 2, 1) * turned[m, 2, t32, :]
            qk[m, r32, :] = w.astype(BF16)
            return 0

        lax.fori_loop(0, ROWS // 32, turn_rows, 0, unroll=2)

    def work_values():
        from_sibling(("F", "YF"))
        project(
            vb,
            lambda: xp[:, 0 : KMAIN + KREM],
            [piece(m, cc, 48) for m in range(2) for cc in range(2)] + [piece(par, 1, 32)],
        )

    def work_permute_values():
        vp[:, 0:512] = dot(vb[...], perm[:, O0 : O0 + 512]).astype(BF16)
        vp[:, 512:1024] = dot(vb[...], perm[:, O0 + 512 : O0 + 1024]).astype(BF16)
        vp[:, 1024:1280] = dot(vb[...], perm[:, HI0 : HI0 + KREM]).astype(BF16)

    def work_attend(h):
        same = (
            lax.rem(lax.broadcasted_iota(jnp.int32, (128, 128), 0), 8)
            == lax.rem(lax.broadcasted_iota(jnp.int32, (128, 128), 1), 8)
        ).astype(F32)
        rows = pl.ds(h * 128, 128)
        num_rem = den_rem = None
        for g in range(4):
            probs = []
            for a in range(4):
                hd = 4 * g + a
                w = (HD * hd) // 128 * 128
                width = min(256, D - w)
                lane = lax.broadcasted_iota(jnp.int32, (16, width), 1) + w
                pick = jnp.logical_and(lane >= HD * hd, lane < HD * (hd + 1)).astype(F32).astype(BF16)
                pick = jnp.concatenate([pick] * 8, axis=0)
                kw = qk[1, rows, w : w + width] * pick
                sc = lax.dot_general(qk[0, rows, w : w + width], kw, (((1,), (1,)), ((), ())), preferred_element_type=F32)
                probs.append((jnp.exp2(sc) * same).astype(BF16))
            p4 = jnp.concatenate(probs, axis=1)
            vg = jnp.concatenate([
                vp[rows, g * 128 : g * 128 + 128],
                vp[rows, 512 + g * 128 : 512 + g * 128 + 128],
                vp[rows, 1024 + (g // 2) * 128 : 1024 + (g // 2) * 128 + 128],
            ], axis=1)
            mk = masks[g % 2]
            num = dot(p4, jnp.concatenate([vg] * 4, axis=0) * mk)
            den = dot(p4, mk)
            inv = 1.0 / den[:, 0:128]
            attp[rows, g * 128 : g * 128 + 128] = (num[:, 0:128] * inv).astype(BF16)
            attp[rows, 512 + g * 128 : 512 + g * 128 + 128] = (num[:, 128:256] * inv).astype(BF16)
            if g % 2 == 0:
                num_rem, den_rem = num[:, 256:384], den[:, 256:384]
            else:
                lo = 1024 + (g // 2) * 128
                attp[rows, lo : lo + 128] = ((num_rem + num[:, 256:384]) / (den_rem + den[:, 256:384])).astype(BF16)

    work = {
        "tab": work_tab,
        "mod": work_mod,
        "rope": work_rope,
        "ln": work_ln,
        "p0": lambda: work_permute(0),
        "p1": lambda: work_permute(1),
        "p2": lambda: work_permute(2),
        "f0": lambda: work_multiply(par, "E"),
        "f1": work_stats,
        "f2": lambda: work_turn(par),
        "g0": lambda: work_multiply(1 - par, "YE"),
        "g1": work_stats,
        "g2": lambda: work_turn(1 - par),
        "v": work_values,
        "vp": work_permute_values,
        "a0": lambda: work_attend(0),
        "a1": lambda: work_attend(1),
    }

    send_onehots()
    for name, hop, *more in SCHEDULE:
        if name in work:
            work[name]()
        elif name not in KINDS:
            send_hidden(name)
        elif hop < 0:
            start_own(name)
        else:
            take(name, hop, more[0] if more else 0)

    from_sibling(("C", "YC"))

    def o_rows(cc):
        return lambda cols: jnp.concatenate([oc[0, cc, :, :, cols], oc[1, cc, :, :, cols]], axis=1).reshape(512, NT)

    project(delta, lambda: attp[...], [o_rows(0), o_rows(1), piece(par, 1, 32)])

    for k in range(NF):
        f = lax.rem(frame + k, NF)
        r16 = pl.ds(pl.multiple_of(f * TOK, TOK), TOK)
        r8 = pl.multiple_of(f * 8, 8)
        gate = modul[2, pl.ds(r8, 8), :]
        both = jnp.concatenate([
            gate * delta[pl.ds(r8, 8), :],
            gate * delta[pl.ds(pl.multiple_of(r8 + 128, 8), 8), :],
        ], axis=0)
        upd[r16, :] = (x_v[r16, :].astype(F32) + both).astype(BF16)
        to_band = band + f // (NF - 1)
        goes = to_band < NB
        if k == NF - 1:
            goes = jnp.logical_and(goes, frame == 0)
            stay = pltpu.make_async_copy(upd.at[r16], out.at[own], local.at[0])

            @pl.when(frame > 0)
            def _():
                stay.start()
                stay.wait()

        pl.when(goes)(functools.partial(push, upd.at[r16], out.at[own], (to_band, lax.rem(f + 1, NF)), 14, FIN))

    some, most = pl.ds(0, ROWS - 2 * TOK), pl.ds(0, ROWS - TOK)
    starts, ends = frame == 0, band == NB - 1
    both_ways = jnp.logical_and
    pl.when(both_ways(starts, band > 0))(lambda: settle(out, rsem=FIN))
    pl.when(frame > 0)(lambda: settle(out.at[most], rsem=FIN))
    pl.when(both_ways(starts, band < NB - 1))(lambda: settle(upd, ssem=14))
    pl.when(starts == ends)(lambda: settle(upd.at[most], ssem=14))
    pl.when(both_ways(frame > 0, ends))(lambda: settle(upd.at[some], ssem=14))
    settle(hidden.at[most], ssem=12)
    settle(onehot.at[pl.ds(0, NF - 1)], ssem=13)
    for n, kind in enumerate(KINDS):
        settle(same_bytes(NF - 1, kind), ssem=n)
        settle(same_bytes(NF - 1, kind), ssem=6 + n)


def local_step(hidden, timesteps, ada_table, w_qkv, w_out, q_gain, k_gain, fresh):
    hbm = pl.BlockSpec(memory_space=pl.ANY)
    consts = constants()
    shapes = [
        pltpu.VMEM((2, 2, 16, 64, D), BF16),
        pltpu.VMEM((2, 2, 16, 16, D), BF16),
        pltpu.VMEM((72, 3 * D), BF16),
        pltpu.VMEM((72, D), BF16),
        pltpu.VMEM((ROWS, D), BF16),
        pltpu.VMEM((3, STEPS, D), F32),
        pltpu.VMEM((3, 128, D), F32),
        pltpu.VMEM((NF, 8, 128), F32),
        *[pltpu.VMEM(a.shape, a.dtype) for a in consts],
        pltpu.VMEM((2, 1, HD), F32),
        pltpu.VMEM((3, 128, D), F32),
        pltpu.VMEM((2, 3, 128, D), F32),
        pltpu.VMEM((ROWS, D), F32),
        pltpu.VMEM((ROWS, D), BF16),
        pltpu.VMEM((ROWS, O0), BF16),
        pltpu.VMEM((ROWS, D), F32),
        pltpu.VMEM((ROWS, D), F32),
        pltpu.VMEM((2, ROWS, D), BF16),
        pltpu.VMEM((ROWS, D), BF16),
        pltpu.VMEM((ROWS, 1280), BF16),
        pltpu.VMEM((ROWS, 1280), BF16),
        pltpu.VMEM((ROWS, D), F32),
        pltpu.VMEM((ROWS, D), BF16),
        pltpu.SemaphoreType.DMA((15,)),
        pltpu.SemaphoreType.DMA((45,)),
        pltpu.SemaphoreType.DMA((12,)),
    ]
    moved = pl.pallas_call(
        kernel,
        out_shape=jax.ShapeDtypeStruct((ROWS, D), BF16),
        in_specs=[hbm, pl.BlockSpec(memory_space=pltpu.SMEM)] + [hbm] * (5 + len(consts)),
        out_specs=hbm,
        scratch_shapes=shapes,
        compiler_params=pltpu.CompilerParams(collective_id=0, has_side_effects=True, vmem_limit_bytes=56 << 20),
        name="queue_step",
    )(hidden[0, 0], timesteps, jnp.transpose(ada_table, (1, 0, 2)), w_qkv, w_out, q_gain[None], k_gain[None], *consts)
    first = jnp.logical_and(lax.axis_index("band") == 0, lax.axis_index("frame") == 0)
    return jnp.where(first, fresh, moved)[None, None]


def solution(mesh):
    return jax.shard_map(
        local_step,
        mesh=mesh,
        in_specs=(
            P("band", "frame", None, None),
            P("band", "frame"),
            P(),
            P("frame", None),
            P("frame", None),
            P(),
            P(),
            P(),
        ),
        out_specs=P("band", "frame", None, None),
        check_vma=False,
    )
```

```python
import functools
import math

import jax
import jax.numpy as jnp
import numpy as np
from jax import lax
from jax.experimental import pallas as pl
from jax.experimental.pallas import tpu as pltpu
from jax.sharding import PartitionSpec as P

MESH = pl.DeviceIdType.MESH
D, HEADS, HD, ROWS, NF, STEPS, NB = 1152, 16, 72, 256, 16, 30, 32
TOK = ROWS // NF
F32, BF16 = jnp.float32, jnp.bfloat16
KMAIN, KREM = 1024, 256
LO0, HI0, O0 = KMAIN, KMAIN + KREM, KMAIN + 2 * KREM
KALL = O0 + KMAIN
KINDS = ("E", "F", "C", "YE", "YF", "YC")
WORK = ("tab", "mod", "rope", "ln", "p0", "p1", "p2", "f0", "f1", "f2", "g0", "g1", "g2", "v", "vp", "a0", "a1")
HOPS = (
    ((-1, 0), (1, 0), (0, -1), (0, 1)),
    ((2, 0), (-1, -1), (-1, 1), (1, 1), (1, -1), (0, 2)),
    ((2, 1), (2, -1), (-1, 2), (1, 2)),
    ((2, 2),),
)
SCHEDULE = (
    ("E", -1), (3, 0), ("F", -1), ("E", 0, 1), ("tab", 0), ("mod", 0), ("rope", 0), ("F", 0),
    ("C", -1), ("E", 1, 1), ("F", 1), ("C", 0), ("E", 2, 1), ("YE", 0), ("F", 2), ("C", 1),
    ("E", 3), ("YE", 1), ("F", 3), ("C", 2), ("ln", 0), ("YE", 2), ("p0", 0), ("YF", 0),
    ("YF", 1), ("YC", 0), ("p1", 0), ("YE", 3), ("p2", 0), ("f0", 0), ("C", 3), ("YF", 2),
    ("YF", 3), ("f1", 0), ("f2", 0), ("YC", 1), ("g0", 0), ("YC", 2), ("g1", 0), ("g2", 0),
    ("v", 0), ("YC", 3), ("vp", 0), ("a0", 0), ("a1", 0),
)


def constants():
    source = np.full((KALL,), -1, np.int64)
    for c in range(2):
        for s in range(16):
            for r in range(32):
                source[O0 + c * 512 + s * 32 + r] = s * HD + c * 32 + r
    for m in range(2):
        for c in range(2):
            for s in range(16):
                for r in range(16):
                    source[(m * 2 + c) * 256 + s * 16 + r] = s * HD + c * 32 + m * 16 + r
    for s in range(16):
        for j in range(8):
            source[LO0 + s * 16 + j] = s * HD + 64 + j
            source[HI0 + s * 16 + 8 + j] = s * HD + 64 + j
    perm = np.zeros((D, KALL), np.float32)
    for n in range(KALL):
        if source[n] >= 0:
            perm[source[n], n] = 1.0
    lane = np.arange(D)
    gather = (lane[:, None] // HD == np.arange(128)[None, :]).astype(np.float32)
    spread = gather.T.copy()
    tile = (lane[None, :] % HD == np.arange(HD)[:, None]).astype(np.float32)
    half = HD // 2
    freq = np.power(10000.0, -2.0 * np.arange(half) / HD).astype(np.float32)
    angle = (np.arange(NF, dtype=np.float32)[:, None] * freq[None, :]).astype(np.float64)
    index = (lane % HD) % half
    first = (lane % HD) < half
    cosine = np.cos(angle)[:, index]
    sine = np.sin(angle)[:, index]
    rope = np.stack([cosine, np.where(first, -sine, 0.0), np.where(first, 0.0, sine)])
    rope = np.repeat(rope, 8, axis=1).astype(np.float32)
    masks = np.zeros((2, 4, 128, 384), np.float32)
    for g in range(2):
        for a in range(4):
            masks[g, a, :, 32 * a : 32 * a + 32] = 1.0
            masks[g, a, :, 128 + 32 * a : 128 + 32 * a + 32] = 1.0
            masks[g, a, :, 256 + 64 * g + 16 * a : 256 + 64 * g + 16 * a + 16] = 1.0
    masks = masks.reshape(2, 512, 384)
    return (
        jnp.asarray(perm, BF16),
        jnp.asarray(gather, BF16),
        jnp.asarray(spread, BF16),
        jnp.asarray(tile, F32),
        jnp.asarray(rope, F32),
        jnp.asarray(masks, BF16),
    )


def dot(a, b, **kw):
    return jnp.dot(a, b, preferred_element_type=F32, **kw)


def kernel(
    hidden, steps, table, wqkv, wout, q_gain, k_gain, perm_h, gather_h, spread_h, tile_h, rope_h, masks_h,
    out,
    eo, oc, wq_v, wo_v, x_v, table_v, tab, onehot, perm, gather, spread, tile, rope, masks, gain_v,
    modul, turned, normed, nb, xp, qf, rf, qk, vb, vp, attp, delta, upd,
    send, recv, local,
):
    band = lax.axis_index("band")
    frame = lax.axis_index("frame")
    c = lax.rem(band, 2)
    y = lax.rem(band // 2, 8)
    par = lax.rem(y, 2)
    z_lo = lax.rem(frame, 4)
    x = frame // 4
    z = (band // 16) * 4 + z_lo

    def device(dx, dy, dz, core):
        xx = lax.rem(x + dx + 4, 4)
        yy = lax.rem(y + dy + 8, 8)
        zz = lax.rem(z + dz + 8, 8)
        return ((zz // 4) * 16 + yy * 2 + core, xx * 4 + lax.rem(zz, 4))

    y_up, y_dn = device(0, 1, 0, c), device(0, -1, 0, c)
    sib = device(0, 0, 0, 1 - c)

    def shard(ax, i, j):
        xx = lax.rem(x + i * ax + j * (1 - ax) + 4, 4)
        zz = lax.rem(z_lo + i * (1 - ax) + j * ax + 4, 4)
        return xx * 4 + zz

    def fetch(src, dst, k):
        cp = pltpu.make_async_copy(src, dst, local.at[k])
        cp.start()
        return cp

    got_w = [fetch(wqkv, wq_v, 0), fetch(wout, wo_v, 1)]
    own = pl.ds(pl.multiple_of(frame * TOK, TOK), TOK)
    got_own = fetch(hidden.at[own], x_v.at[own], 2)
    got_tab = fetch(table, table_v, 3)
    got_rest = [
        fetch(a, b, 4 + k)
        for k, (a, b) in enumerate(
            ((perm_h, perm), (gather_h, gather), (spread_h, spread), (tile_h, tile), (rope_h, rope), (masks_h, masks), (q_gain, gain_v.at[0]), (k_gain, gain_v.at[1]))
        )
    ]

    barrier = pltpu.get_barrier_semaphore()

    def greet(d):
        pl.semaphore_signal(barrier, inc=1, device_id=d, device_id_type=MESH)

    for move in ((1, 0, 0), (-1, 0, 0), (0, 1, 0), (0, -1, 0), (0, 0, 1), (0, 0, -1)):
        greet(device(*move, c))
    greet(sib)
    for k in range(1, NF):
        greet((band, lax.rem(frame + k, NF)))

    @pl.when(jnp.logical_and(frame == 0, band > 0))
    def _():
        for k in range(NF):
            greet((band - 1, k))

    for cp in got_w:
        cp.wait()
    me = frame
    rest = wq_v[64:72, :].astype(F32)
    rest_o = wo_v[64:72, :].astype(F32)
    tails = (
        jnp.concatenate([rest[:, 0:D], rest[:, D : 2 * D]], axis=0).astype(BF16),
        jnp.concatenate([rest[:, 2 * D :], rest_o], axis=0).astype(BF16),
    )
    for cc in range(2):
        for m in range(2):
            eo[m, cc, me, 0:32, :] = wq_v[32 * cc : 32 * cc + 32, m * D : (m + 1) * D]
            eo[m, cc, me, 32:48, :] = tails[cc]
            eo[m, cc, me, 48:64, :] = wq_v[32 * cc + 16 * m : 32 * cc + 16 * m + 16, 2 * D :]
            oc[m, cc, me] = wo_v[32 * cc + 16 * m : 32 * cc + 16 * m + 16, :]

    pl.semaphore_wait(barrier, 22 + lax.min(NB - 1 - band, 1))

    def push(src, dst, d, ssem, rsem):
        pltpu.make_async_remote_copy(src, dst, send.at[ssem], recv.at[rsem], device_id=d, device_id_type=MESH).start()

    def settle(ref, ssem=None, rsem=None):
        cp = pltpu.make_async_remote_copy(ref, ref, send.at[ssem or 0], recv.at[rsem or 0], device_id=sib, device_id_type=MESH)
        if rsem is None:
            cp.wait_send()
        else:
            cp.wait_recv()

    SPAN = {"E": (0, 48), "F": (48, 16), "YE": (0, 32), "YF": (48, 16), "C": (0, 16), "YC": (0, 16)}

    def block(kind, i, j):
        which = shard(FIRST_X[kind[-1]], i, j)
        m = 1 - par if kind[0] == "Y" else par
        if kind[-1] == "C":
            return oc.at[m, c, which]
        start, size = SPAN[kind]
        return eo.at[m, c, which, pl.ds(start, size)]

    def same_bytes(count, kind):
        return eo.at[0, 0, pl.ds(0, count), pl.ds(0, SPAN[kind][1])]

    def hop_of(i, j):
        return [n for n, hop in enumerate(HOPS) if (i, j) in hop][0]

    def slot(kind, i, j):
        if kind == "E":
            return 4 * i + j + 5
        return 16 + 4 * (KINDS.index(kind) - 1) + hop_of(i, j)

    SIB, HID, HOT, FIN = 36, 42, 43, 44

    def push_block(kind, i, j, d, ri, rj):
        ref = block(kind, i, j)
        push(ref, ref, d, KINDS.index(kind), slot(kind, ri, rj))

    FIRST_X = {"E": 1 - c, "F": 1 - c, "C": 0}

    def ways(kind):
        ax = FIRST_X[kind]
        return device(ax, 0, 1 - ax, c), device(-ax, 0, ax - 1, c), device(1 - ax, 0, ax, c), device(ax - 1, 0, -ax, c)

    WAYS = {kind: ways(kind) for kind in FIRST_X}

    def start_own(kind):
        a_up, a_dn, b_up, b_dn = WAYS[kind]
        push_block(kind, 0, 0, b_up, 0, -1)
        push_block(kind, 0, 0, b_dn, 0, 1)
        push_block(kind, 0, 0, a_up, -1, 0)
        push_block(kind, 0, 0, a_dn, 1, 0)

    turn = [0]

    def forward(kind, i, j):
        if kind[0] != "Y":
            a_up, a_dn, b_up, b_dn = WAYS[kind]
            if j == 0:
                if kind != "C" and i == -1:
                    push_block(kind, i, j, a_up, 2, 0)
                if kind == "C" and i == 1:
                    push_block(kind, i, j, a_dn, 2, 0)
                push_block(kind, i, j, b_up, i, -1)
                push_block(kind, i, j, b_dn, i, 1)
            elif j == -1 and i in (0, -1):
                push_block(kind, i, j, b_up, i, 2)
            elif j == 1 and i in (1, 2):
                push_block(kind, i, j, b_dn, i, 2)
            ref = block(kind, i, j)
            if kind == "E":
                ref = eo.at[par, c, shard(FIRST_X[kind], i, j), pl.ds(0, 32)]
            other = "Y" + kind
            push(ref, ref, y_up if turn[0] % 2 == 0 else y_dn, KINDS.index(other), slot(other, i, j))
            turn[0] += 1
        ref = block(kind, i, j)
        push(ref, ref, sib, 6 + KINDS.index(kind), SIB + KINDS.index(kind))

    def take(kind, hop, hidden_after):
        blocks = HOPS[hop]
        if kind != "E":
            settle(same_bytes(len(blocks), kind), rsem=slot(kind, *blocks[0]))
        for i, j in blocks:
            if kind == "E":
                settle(block(kind, i, j), rsem=slot(kind, i, j))
            forward(kind, i, j)
            send_hidden(hidden_after)

    def from_sibling(kinds):
        for kind in kinds:
            settle(same_bytes(NF - 1, kind), rsem=SIB + KINDS.index(kind))

    step = steps[0, 0]
    lanes = lax.broadcasted_iota(jnp.int32, (8, 128), 1)
    onehot[frame] = (lanes == step).astype(F32)
    def send_onehots():
        for k in range(1, NF):
            to = lax.rem(frame + k, NF)
            push(onehot.at[frame], onehot.at[frame], (band, to), 13, HOT)

    far_first = [(dx, dz) for dz in (2, 3, 1, 0) for dx in (2, 1, 3, 0)]
    todo = far_first[:-1]

    def partner(dx, dz):
        return lax.rem(x + dx, 4) * 4 + lax.rem(z_lo + dz, 4)


    def send_hidden(count):
        for _ in range(min(count, len(todo))):
            to = partner(*todo.pop(0))
            rows = pl.ds(pl.multiple_of(to * TOK, TOK), TOK)
            push(hidden.at[rows], x_v.at[own], (band, to), 12, HID)

    NT = D

    def project(dst, lhs, rhs):
        cols = pl.ds(0, NT)
        dst[...] = dot(lhs(), jnp.concatenate([r(cols) for r in rhs], axis=0)).astype(dst.dtype)

    def piece(m, cc, lo):
        return lambda cols: eo[m, cc, :, lo : lo + 16, cols].reshape(256, NT)

    factor = math.log2(math.e) / math.sqrt(HD)

    def work_tab():
        got_tab.wait()
        tab[...] = jnp.zeros_like(tab)
        for j in range(3):
            tab[j, 0:STEPS, :] = table_v[j]

    def work_mod():
        settle(onehot.at[pl.ds(0, NF - 1)], rsem=HOT)
        oh = onehot[...].reshape(128, 128)
        for j in range(3):
            modul[j] = dot(oh, tab[j], precision=lax.Precision.HIGHEST)

    def work_rope():
        for cp in got_rest:
            cp.wait()
        for m in range(2):
            g = dot(jnp.broadcast_to(gain_v[m], (8, HD)), tile[...], precision=lax.Precision.HIGHEST)
            if m == 0:
                g = g * factor
            rolled = (g, pltpu.roll(g, D - HD // 2, 1), pltpu.roll(g, HD // 2, 1))
            for j in range(3):
                turned[m, j] = rope[j] * rolled[j][0:1, :]

    def norm_frame(f, _):
        r16 = pl.ds(pl.multiple_of(f * TOK, TOK), TOK)
        r8 = pl.multiple_of(f * 8, 8)
        v = x_v[r16, :].astype(F32)
        mean = jnp.mean(v, axis=-1, keepdims=True)
        cen = v - mean
        var = jnp.mean(cen * cen, axis=-1, keepdims=True)
        cen = cen * lax.rsqrt(var + 1e-06)
        scale = 1.0 + modul[1, pl.ds(r8, 8), :]
        shift = modul[0, pl.ds(r8, 8), :]
        normed[pl.ds(r8, 8), :] = cen[0:8] * scale + shift
        normed[pl.ds(pl.multiple_of(r8 + 128, 8), 8), :] = cen[8:16] * scale + shift
        return 0

    def work_ln():
        got_own.wait()
        settle(x_v.at[pl.ds(0, ROWS - TOK)], rsem=HID)
        lax.fori_loop(0, NF, norm_frame, 0, unroll=8)
        nb[...] = normed[...].astype(BF16)

    def work_permute(n):
        cols = pl.ds(n * 512, 512)
        xp[:, cols] = dot(nb[...], perm[:, cols]).astype(BF16)

    def work_multiply(m, kind):
        from_sibling((kind,))
        last = pl.ds(pl.multiple_of(LO0 + KREM * m, KREM), KREM)
        project(
            qf,
            lambda: jnp.concatenate([xp[:, 0:KMAIN], xp[:, last]], axis=1),
            [piece(m, cc, 16 * half) for half in range(2) for cc in range(2)] + [piece(par, 0, 32)],
        )

    def work_stats():
        squares = qf[...]
        ss = dot((squares * squares).astype(BF16), gather[...])
        r = lax.rsqrt(ss * (1.0 / HD) + 1e-06)
        hi = r.astype(BF16)
        lo = (r - hi.astype(F32)).astype(BF16)
        rf[...] = dot(jnp.concatenate([hi, lo], axis=1), jnp.concatenate([spread[...], spread[...]], axis=0))

    def work_turn(m):
        def turn_rows(g, _):
            r32 = pl.ds(pl.multiple_of(g * 32, 32), 32)
            t32 = pl.ds(pl.multiple_of(lax.rem(g, 4) * 32, 32), 32)
            v = qf[r32, :] * rf[r32, :]
            w = v * turned[m, 0, t32, :]
            w = w + pltpu.roll(v, D - HD // 2, 1) * turned[m, 1, t32, :]
            w = w + pltpu.roll(v, HD // 2, 1) * turned[m, 2, t32, :]
            qk[m, r32, :] = w.astype(BF16)
            return 0

        lax.fori_loop(0, ROWS // 32, turn_rows, 0, unroll=2)

    def work_values():
        from_sibling(("F", "YF"))
        project(
            vb,
            lambda: xp[:, 0 : KMAIN + KREM],
            [piece(m, cc, 48) for m in range(2) for cc in range(2)] + [piece(par, 1, 32)],
        )

    def work_permute_values():
        vp[:, 0:512] = dot(vb[...], perm[:, O0 : O0 + 512]).astype(BF16)
        vp[:, 512:1024] = dot(vb[...], perm[:, O0 + 512 : O0 + 1024]).astype(BF16)
        vp[:, 1024:1280] = dot(vb[...], perm[:, HI0 : HI0 + KREM]).astype(BF16)

    def work_attend(h):
        same = (
            lax.rem(lax.broadcasted_iota(jnp.int32, (128, 128), 0), 8)
            == lax.rem(lax.broadcasted_iota(jnp.int32, (128, 128), 1), 8)
        ).astype(F32)
        rows = pl.ds(h * 128, 128)
        num_rem = den_rem = None
        for g in range(4):
            probs = []
            for a in range(4):
                hd = 4 * g + a
                w = (HD * hd) // 128 * 128
                width = min(256, D - w)
                lane = lax.broadcasted_iota(jnp.int32, (16, width), 1) + w
                pick = jnp.logical_and(lane >= HD * hd, lane < HD * (hd + 1)).astype(F32).astype(BF16)
                pick = jnp.concatenate([pick] * 8, axis=0)
                kw = qk[1, rows, w : w + width] * pick
                sc = lax.dot_general(qk[0, rows, w : w + width], kw, (((1,), (1,)), ((), ())), preferred_element_type=F32)
                probs.append((jnp.exp2(sc) * same).astype(BF16))
            p4 = jnp.concatenate(probs, axis=1)
            vg = jnp.concatenate([
                vp[rows, g * 128 : g * 128 + 128],
                vp[rows, 512 + g * 128 : 512 + g * 128 + 128],
                vp[rows, 1024 + (g // 2) * 128 : 1024 + (g // 2) * 128 + 128],
            ], axis=1)
            mk = masks[g % 2]
            num = dot(p4, jnp.concatenate([vg] * 4, axis=0) * mk)
            den = dot(p4, mk)
            inv = 1.0 / den[:, 0:128]
            attp[rows, g * 128 : g * 128 + 128] = (num[:, 0:128] * inv).astype(BF16)
            attp[rows, 512 + g * 128 : 512 + g * 128 + 128] = (num[:, 128:256] * inv).astype(BF16)
            if g % 2 == 0:
                num_rem, den_rem = num[:, 256:384], den[:, 256:384]
            else:
                lo = 1024 + (g // 2) * 128
                attp[rows, lo : lo + 128] = ((num_rem + num[:, 256:384]) / (den_rem + den[:, 256:384])).astype(BF16)

    work = {
        "tab": work_tab,
        "mod": work_mod,
        "rope": work_rope,
        "ln": work_ln,
        "p0": lambda: work_permute(0),
        "p1": lambda: work_permute(1),
        "p2": lambda: work_permute(2),
        "f0": lambda: work_multiply(par, "E"),
        "f1": work_stats,
        "f2": lambda: work_turn(par),
        "g0": lambda: work_multiply(1 - par, "YE"),
        "g1": work_stats,
        "g2": lambda: work_turn(1 - par),
        "v": work_values,
        "vp": work_permute_values,
        "a0": lambda: work_attend(0),
        "a1": lambda: work_attend(1),
    }

    send_onehots()
    for name, hop, *more in SCHEDULE:
        if name in work:
            work[name]()
        elif name not in KINDS:
            send_hidden(name)
        elif hop < 0:
            start_own(name)
        else:
            take(name, hop, more[0] if more else 0)

    from_sibling(("C", "YC"))

    def o_rows(cc):
        return lambda cols: jnp.concatenate([oc[0, cc, :, :, cols], oc[1, cc, :, :, cols]], axis=1).reshape(512, NT)

    project(delta, lambda: attp[...], [o_rows(0), o_rows(1), piece(par, 1, 32)])

    for place in far_first:
        to_frame = partner(*place)
        f = lax.rem(to_frame + NF - 1, NF)
        r16 = pl.ds(pl.multiple_of(f * TOK, TOK), TOK)
        r8 = pl.multiple_of(f * 8, 8)
        gate = modul[2, pl.ds(r8, 8), :]
        both = jnp.concatenate([
            gate * delta[pl.ds(r8, 8), :],
            gate * delta[pl.ds(pl.multiple_of(r8 + 128, 8), 8), :],
        ], axis=0)
        upd[r16, :] = (x_v[r16, :].astype(F32) + both).astype(BF16)
        to_band = band + f // (NF - 1)
        goes = to_band < NB
        if place == (0, 0):
            goes = jnp.logical_and(goes, frame == 0)
            stay = pltpu.make_async_copy(upd.at[r16], out.at[own], local.at[0])

            @pl.when(frame > 0)
            def _():
                stay.start()
                stay.wait()

        pl.when(goes)(functools.partial(push, upd.at[r16], out.at[own], (to_band, to_frame), 14, FIN))

    some, most = pl.ds(0, ROWS - 2 * TOK), pl.ds(0, ROWS - TOK)
    starts, ends = frame == 0, band == NB - 1
    both_ways = jnp.logical_and
    pl.when(both_ways(starts, band > 0))(lambda: settle(out, rsem=FIN))
    pl.when(frame > 0)(lambda: settle(out.at[most], rsem=FIN))
    pl.when(both_ways(starts, band < NB - 1))(lambda: settle(upd, ssem=14))
    pl.when(starts == ends)(lambda: settle(upd.at[most], ssem=14))
    pl.when(both_ways(frame > 0, ends))(lambda: settle(upd.at[some], ssem=14))
    settle(hidden.at[most], ssem=12)
    settle(onehot.at[pl.ds(0, NF - 1)], ssem=13)
    for n, kind in enumerate(KINDS):
        settle(same_bytes(NF - 1, kind), ssem=n)
        settle(same_bytes(NF - 1, kind), ssem=6 + n)


def local_step(hidden, timesteps, ada_table, w_qkv, w_out, q_gain, k_gain, fresh):
    hbm = pl.BlockSpec(memory_space=pl.ANY)
    consts = constants()
    shapes = [
        pltpu.VMEM((2, 2, 16, 64, D), BF16),
        pltpu.VMEM((2, 2, 16, 16, D), BF16),
        pltpu.VMEM((72, 3 * D), BF16),
        pltpu.VMEM((72, D), BF16),
        pltpu.VMEM((ROWS, D), BF16),
        pltpu.VMEM((3, STEPS, D), F32),
        pltpu.VMEM((3, 128, D), F32),
        pltpu.VMEM((NF, 8, 128), F32),
        *[pltpu.VMEM(a.shape, a.dtype) for a in consts],
        pltpu.VMEM((2, 1, HD), F32),
        pltpu.VMEM((3, 128, D), F32),
        pltpu.VMEM((2, 3, 128, D), F32),
        pltpu.VMEM((ROWS, D), F32),
        pltpu.VMEM((ROWS, D), BF16),
        pltpu.VMEM((ROWS, O0), BF16),
        pltpu.VMEM((ROWS, D), F32),
        pltpu.VMEM((ROWS, D), F32),
        pltpu.VMEM((2, ROWS, D), BF16),
        pltpu.VMEM((ROWS, D), BF16),
        pltpu.VMEM((ROWS, 1280), BF16),
        pltpu.VMEM((ROWS, 1280), BF16),
        pltpu.VMEM((ROWS, D), F32),
        pltpu.VMEM((ROWS, D), BF16),
        pltpu.SemaphoreType.DMA((15,)),
        pltpu.SemaphoreType.DMA((45,)),
        pltpu.SemaphoreType.DMA((12,)),
    ]
    moved = pl.pallas_call(
        kernel,
        out_shape=jax.ShapeDtypeStruct((ROWS, D), BF16),
        in_specs=[hbm, pl.BlockSpec(memory_space=pltpu.SMEM)] + [hbm] * (5 + len(consts)),
        out_specs=hbm,
        scratch_shapes=shapes,
        compiler_params=pltpu.CompilerParams(collective_id=0, has_side_effects=True, vmem_limit_bytes=56 << 20),
        name="queue_step",
    )(hidden[0, 0], timesteps, jnp.transpose(ada_table, (1, 0, 2)), w_qkv, w_out, q_gain[None], k_gain[None], *consts)
    first = jnp.logical_and(lax.axis_index("band") == 0, lax.axis_index("frame") == 0)
    return jnp.where(first, fresh, moved)[None, None]


def solution(mesh):
    return jax.shard_map(
        local_step,
        mesh=mesh,
        in_specs=(
            P("band", "frame", None, None),
            P("band", "frame"),
            P(),
            P("frame", None),
            P("frame", None),
            P(),
            P(),
            P(),
        ),
        out_specs=P("band", "frame", None, None),
        check_vma=False,
    )
```

```python
import functools
import math

import jax
import jax.numpy as jnp
import numpy as np
from jax import lax
from jax.experimental import pallas as pl
from jax.experimental.pallas import tpu as pltpu
from jax.sharding import PartitionSpec as P

MESH = pl.DeviceIdType.MESH
D, HEADS, HD, ROWS, NF, STEPS, NB = 1152, 16, 72, 256, 16, 30, 32
TOK = ROWS // NF
F32, BF16 = jnp.float32, jnp.bfloat16
KMAIN, KREM = 1024, 256
LO0, HI0, O0 = KMAIN, KMAIN + KREM, KMAIN + 2 * KREM
KALL = O0 + KMAIN
KINDS = ("E", "F", "C", "YE", "YF", "YC")
WORK = ("tab", "mod", "rope", "ln", "p0", "p1", "p2", "f0", "f1", "f2", "g0", "g1", "g2", "v", "vp", "a0", "a1")
HOPS = (
    ((-1, 0), (1, 0), (0, -1), (0, 1)),
    ((2, 0), (-1, -1), (-1, 1), (1, 1), (1, -1), (0, 2)),
    ((2, 1), (2, -1), (-1, 2), (1, 2)),
    ((2, 2),),
)
SCHEDULE = (
    ("E", -1), ("F", -1), ("C", -1), (3, 0), ("E", 0, 1), ("F", 0), ("C", 0), ("tab", 0),
    ("mod", 0), ("E", 1, 1), ("YE", 0), ("F", 1), ("YF", 0), ("C", 1), ("YC", 0), ("rope", 0),
    ("E", 2, 1), ("F", 2), ("C", 2), ("YE", 1), ("YF", 1), ("YC", 1), ("E", 3), ("F", 3),
    ("C", 3), ("ln", 0), ("YE", 2), ("p0", 0), ("YF", 2), ("YC", 2), ("p1", 0), ("YE", 3),
    ("p2", 0), ("YF", 3), ("YC", 3), ("f0", 0), ("f1", 0), ("f2", 0), ("g0", 0), ("g1", 0),
    ("g2", 0), ("v", 0), ("vp", 0), ("a0", 0), ("a1", 0),
)


def constants():
    source = np.full((KALL,), -1, np.int64)
    for c in range(2):
        for s in range(16):
            for r in range(32):
                source[O0 + c * 512 + s * 32 + r] = s * HD + c * 32 + r
    for m in range(2):
        for c in range(2):
            for s in range(16):
                for r in range(16):
                    source[(m * 2 + c) * 256 + s * 16 + r] = s * HD + c * 32 + m * 16 + r
    for s in range(16):
        for j in range(8):
            source[LO0 + s * 16 + j] = s * HD + 64 + j
            source[HI0 + s * 16 + 8 + j] = s * HD + 64 + j
    perm = np.zeros((D, KALL), np.float32)
    for n in range(KALL):
        if source[n] >= 0:
            perm[source[n], n] = 1.0
    lane = np.arange(D)
    gather = (lane[:, None] // HD == np.arange(128)[None, :]).astype(np.float32)
    spread = gather.T.copy()
    tile = (lane[None, :] % HD == np.arange(HD)[:, None]).astype(np.float32)
    half = HD // 2
    freq = np.power(10000.0, -2.0 * np.arange(half) / HD).astype(np.float32)
    angle = (np.arange(NF, dtype=np.float32)[:, None] * freq[None, :]).astype(np.float64)
    index = (lane % HD) % half
    first = (lane % HD) < half
    cosine = np.cos(angle)[:, index]
    sine = np.sin(angle)[:, index]
    rope = np.stack([cosine, np.where(first, -sine, 0.0), np.where(first, 0.0, sine)])
    rope = np.repeat(rope, 8, axis=1).astype(np.float32)
    masks = np.zeros((2, 4, 128, 384), np.float32)
    for g in range(2):
        for a in range(4):
            masks[g, a, :, 32 * a : 32 * a + 32] = 1.0
            masks[g, a, :, 128 + 32 * a : 128 + 32 * a + 32] = 1.0
            masks[g, a, :, 256 + 64 * g + 16 * a : 256 + 64 * g + 16 * a + 16] = 1.0
    masks = masks.reshape(2, 512, 384)
    return (
        jnp.asarray(perm, BF16),
        jnp.asarray(gather, BF16),
        jnp.asarray(spread, BF16),
        jnp.asarray(tile, F32),
        jnp.asarray(rope, F32),
        jnp.asarray(masks, BF16),
    )


def dot(a, b, **kw):
    return jnp.dot(a, b, preferred_element_type=F32, **kw)


def kernel(
    hidden, steps, table, wqkv, wout, q_gain, k_gain, perm_h, gather_h, spread_h, tile_h, rope_h, masks_h,
    out,
    eo, oc, wq_v, wo_v, x_v, table_v, tab, onehot, perm, gather, spread, tile, rope, masks, gain_v,
    modul, turned, normed, nb, xp, qf, rf, qk, vb, vp, attp, delta, upd,
    send, recv, local,
):
    band = lax.axis_index("band")
    frame = lax.axis_index("frame")
    c = lax.rem(band, 2)
    y = lax.rem(band // 2, 8)
    par = lax.rem(y, 2)
    z_lo = lax.rem(frame, 4)
    x = frame // 4
    z = (band // 16) * 4 + z_lo

    def device(dx, dy, dz, core):
        xx = lax.rem(x + dx + 4, 4)
        yy = lax.rem(y + dy + 8, 8)
        zz = lax.rem(z + dz + 8, 8)
        return ((zz // 4) * 16 + yy * 2 + core, xx * 4 + lax.rem(zz, 4))

    y_up, y_dn = device(0, 1, 0, c), device(0, -1, 0, c)
    sib = device(0, 0, 0, 1 - c)

    def shard(ax, i, j):
        xx = lax.rem(x + i * ax + j * (1 - ax) + 4, 4)
        zz = lax.rem(z_lo + i * (1 - ax) + j * ax + 4, 4)
        return xx * 4 + zz

    def fetch(src, dst, k):
        cp = pltpu.make_async_copy(src, dst, local.at[k])
        cp.start()
        return cp

    got_w = [fetch(wqkv, wq_v, 0), fetch(wout, wo_v, 1)]
    own = pl.ds(pl.multiple_of(frame * TOK, TOK), TOK)
    got_own = fetch(hidden.at[own], x_v.at[own], 2)
    got_tab = fetch(table, table_v, 3)
    got_rest = [
        fetch(a, b, 4 + k)
        for k, (a, b) in enumerate(
            ((tile_h, tile), (rope_h, rope), (q_gain, gain_v.at[0]), (k_gain, gain_v.at[1]), (perm_h, perm), (gather_h, gather), (spread_h, spread), (masks_h, masks))
        )
    ]

    barrier = pltpu.get_barrier_semaphore()

    def greet(d):
        pl.semaphore_signal(barrier, inc=1, device_id=d, device_id_type=MESH)

    for move in ((1, 0, 0), (-1, 0, 0), (0, 1, 0), (0, -1, 0), (0, 0, 1), (0, 0, -1)):
        greet(device(*move, c))
    greet(sib)
    for k in range(1, NF):
        greet((band, lax.rem(frame + k, NF)))

    @pl.when(jnp.logical_and(frame == 0, band > 0))
    def _():
        for k in range(NF):
            greet((band - 1, k))

    for cp in got_w:
        cp.wait()
    me = frame
    rest = wq_v[64:72, :].astype(F32)
    rest_o = wo_v[64:72, :].astype(F32)
    tails = (
        jnp.concatenate([rest[:, 0:D], rest[:, D : 2 * D]], axis=0).astype(BF16),
        jnp.concatenate([rest[:, 2 * D :], rest_o], axis=0).astype(BF16),
    )
    for cc in range(2):
        for m in range(2):
            eo[m, cc, me, 0:32, :] = wq_v[32 * cc : 32 * cc + 32, m * D : (m + 1) * D]
            eo[m, cc, me, 32:48, :] = tails[cc]
            eo[m, cc, me, 48:64, :] = wq_v[32 * cc + 16 * m : 32 * cc + 16 * m + 16, 2 * D :]
            oc[m, cc, me] = wo_v[32 * cc + 16 * m : 32 * cc + 16 * m + 16, :]

    pl.semaphore_wait(barrier, 22 + lax.min(NB - 1 - band, 1))

    def push(src, dst, d, ssem, rsem):
        pltpu.make_async_remote_copy(src, dst, send.at[ssem], recv.at[rsem], device_id=d, device_id_type=MESH).start()

    def settle(ref, ssem=None, rsem=None):
        cp = pltpu.make_async_remote_copy(ref, ref, send.at[ssem or 0], recv.at[rsem or 0], device_id=sib, device_id_type=MESH)
        if rsem is None:
            cp.wait_send()
        else:
            cp.wait_recv()

    SPAN = {"E": (0, 48), "F": (48, 16), "YE": (0, 32), "YF": (48, 16), "C": (0, 16), "YC": (0, 16)}

    def block(kind, i, j):
        which = shard(FIRST_X[kind[-1]], i, j)
        m = 1 - par if kind[0] == "Y" else par
        if kind[-1] == "C":
            return oc.at[m, c, which]
        start, size = SPAN[kind]
        return eo.at[m, c, which, pl.ds(start, size)]

    def same_bytes(count, kind):
        return eo.at[0, 0, pl.ds(0, count), pl.ds(0, SPAN[kind][1])]

    def hop_of(i, j):
        return [n for n, hop in enumerate(HOPS) if (i, j) in hop][0]

    def slot(kind, i, j):
        if kind == "E":
            return 4 * i + j + 5
        return 16 + 4 * (KINDS.index(kind) - 1) + hop_of(i, j)

    SIB, HID, HOT, FIN = 36, 42, 43, 44

    def push_block(kind, i, j, d, ri, rj):
        ref = block(kind, i, j)
        push(ref, ref, d, KINDS.index(kind), slot(kind, ri, rj))

    FIRST_X = {"E": 1 - c, "F": 1 - c, "C": 0}

    def ways(kind):
        ax = FIRST_X[kind]
        return device(ax, 0, 1 - ax, c), device(-ax, 0, ax - 1, c), device(1 - ax, 0, ax, c), device(ax - 1, 0, -ax, c)

    WAYS = {kind: ways(kind) for kind in FIRST_X}

    def start_own(kind):
        a_up, a_dn, b_up, b_dn = WAYS[kind]
        push_block(kind, 0, 0, b_up, 0, -1)
        push_block(kind, 0, 0, b_dn, 0, 1)
        push_block(kind, 0, 0, a_up, -1, 0)
        push_block(kind, 0, 0, a_dn, 1, 0)

    turn = [0]

    def forward(kind, i, j):
        if kind[0] != "Y":
            a_up, a_dn, b_up, b_dn = WAYS[kind]
            if j == 0:
                if kind != "C" and i == -1:
                    push_block(kind, i, j, a_up, 2, 0)
                if kind == "C" and i == 1:
                    push_block(kind, i, j, a_dn, 2, 0)
                push_block(kind, i, j, b_up, i, -1)
                push_block(kind, i, j, b_dn, i, 1)
            elif j == -1 and i in (0, -1):
                push_block(kind, i, j, b_up, i, 2)
            elif j == 1 and i in (1, 2):
                push_block(kind, i, j, b_dn, i, 2)
            ref = block(kind, i, j)
            if kind == "E":
                ref = eo.at[par, c, shard(FIRST_X[kind], i, j), pl.ds(0, 32)]
            other = "Y" + kind
            push(ref, ref, y_up if turn[0] % 2 == 0 else y_dn, KINDS.index(other), slot(other, i, j))
            turn[0] += 1
        ref = block(kind, i, j)
        push(ref, ref, sib, 6 + KINDS.index(kind), SIB + KINDS.index(kind))

    def take(kind, hop, hidden_after):
        blocks = HOPS[hop]
        if kind != "E":
            settle(same_bytes(len(blocks), kind), rsem=slot(kind, *blocks[0]))
        for i, j in blocks:
            if kind == "E":
                settle(block(kind, i, j), rsem=slot(kind, i, j))
            forward(kind, i, j)
            send_hidden(hidden_after)

    def from_sibling(kinds):
        for kind in kinds:
            settle(same_bytes(NF - 1, kind), rsem=SIB + KINDS.index(kind))

    step = steps[0, 0]
    lanes = lax.broadcasted_iota(jnp.int32, (8, 128), 1)
    onehot[frame] = (lanes == step).astype(F32)
    def send_onehots():
        for k in range(1, NF):
            to = lax.rem(frame + k, NF)
            push(onehot.at[frame], onehot.at[frame], (band, to), 13, HOT)

    far_first = [(dx, dz) for dz in (2, 3, 1, 0) for dx in (2, 1, 3, 0)]
    todo = far_first[:-1]

    def partner(dx, dz):
        return lax.rem(x + dx, 4) * 4 + lax.rem(z_lo + dz, 4)


    def send_hidden(count):
        for _ in range(min(count, len(todo))):
            to = partner(*todo.pop(0))
            rows = pl.ds(pl.multiple_of(to * TOK, TOK), TOK)
            push(hidden.at[rows], x_v.at[own], (band, to), 12, HID)

    NT = D

    def project(dst, lhs, rhs):
        cols = pl.ds(0, NT)
        dst[...] = dot(lhs(), jnp.concatenate([r(cols) for r in rhs], axis=0)).astype(dst.dtype)

    def piece(m, cc, lo):
        return lambda cols: eo[m, cc, :, lo : lo + 16, cols].reshape(256, NT)

    factor = math.log2(math.e) / math.sqrt(HD)

    def work_tab():
        got_tab.wait()
        tab[...] = jnp.zeros_like(tab)
        for j in range(3):
            tab[j, 0:STEPS, :] = table_v[j]

    def work_mod():
        settle(onehot.at[pl.ds(0, NF - 1)], rsem=HOT)
        oh = onehot[...].reshape(128, 128)
        for j in range(3):
            modul[j] = dot(oh, tab[j], precision=lax.Precision.HIGHEST)

    def work_rope():
        for cp in got_rest[:4]:
            cp.wait()
        for m in range(2):
            g = dot(jnp.broadcast_to(gain_v[m], (8, HD)), tile[...], precision=lax.Precision.HIGHEST)
            if m == 0:
                g = g * factor
            rolled = (g, pltpu.roll(g, D - HD // 2, 1), pltpu.roll(g, HD // 2, 1))
            for j in range(3):
                turned[m, j] = rope[j] * rolled[j][0:1, :]

    def norm_frame(f, _):
        r16 = pl.ds(pl.multiple_of(f * TOK, TOK), TOK)
        r8 = pl.multiple_of(f * 8, 8)
        v = x_v[r16, :].astype(F32)
        mean = jnp.mean(v, axis=-1, keepdims=True)
        cen = v - mean
        var = jnp.mean(cen * cen, axis=-1, keepdims=True)
        cen = cen * lax.rsqrt(var + 1e-06)
        scale = 1.0 + modul[1, pl.ds(r8, 8), :]
        shift = modul[0, pl.ds(r8, 8), :]
        normed[pl.ds(r8, 8), :] = cen[0:8] * scale + shift
        normed[pl.ds(pl.multiple_of(r8 + 128, 8), 8), :] = cen[8:16] * scale + shift
        return 0

    def work_ln():
        for cp in got_rest[4:]:
            cp.wait()
        got_own.wait()
        settle(x_v.at[pl.ds(0, ROWS - TOK)], rsem=HID)
        lax.fori_loop(0, NF, norm_frame, 0, unroll=8)
        nb[...] = normed[...].astype(BF16)

    def work_permute(n):
        cols = pl.ds(n * 512, 512)
        xp[:, cols] = dot(nb[...], perm[:, cols]).astype(BF16)

    def work_multiply(m, kind):
        from_sibling((kind,))
        last = pl.ds(pl.multiple_of(LO0 + KREM * m, KREM), KREM)
        project(
            qf,
            lambda: jnp.concatenate([xp[:, 0:KMAIN], xp[:, last]], axis=1),
            [piece(m, cc, 16 * half) for half in range(2) for cc in range(2)] + [piece(par, 0, 32)],
        )

    def work_stats():
        squares = qf[...]
        ss = dot((squares * squares).astype(BF16), gather[...])
        r = lax.rsqrt(ss * (1.0 / HD) + 1e-06)
        hi = r.astype(BF16)
        lo = (r - hi.astype(F32)).astype(BF16)
        rf[...] = dot(jnp.concatenate([hi, lo], axis=1), jnp.concatenate([spread[...], spread[...]], axis=0))

    def work_turn(m):
        def turn_rows(g, _):
            r32 = pl.ds(pl.multiple_of(g * 32, 32), 32)
            t32 = pl.ds(pl.multiple_of(lax.rem(g, 4) * 32, 32), 32)
            v = qf[r32, :] * rf[r32, :]
            w = v * turned[m, 0, t32, :]
            w = w + pltpu.roll(v, D - HD // 2, 1) * turned[m, 1, t32, :]
            w = w + pltpu.roll(v, HD // 2, 1) * turned[m, 2, t32, :]
            qk[m, r32, :] = w.astype(BF16)
            return 0

        lax.fori_loop(0, ROWS // 32, turn_rows, 0, unroll=2)

    def work_values():
        from_sibling(("F", "YF"))
        project(
            vb,
            lambda: xp[:, 0 : KMAIN + KREM],
            [piece(m, cc, 48) for m in range(2) for cc in range(2)] + [piece(par, 1, 32)],
        )

    def work_permute_values():
        vp[:, 0:512] = dot(vb[...], perm[:, O0 : O0 + 512]).astype(BF16)
        vp[:, 512:1024] = dot(vb[...], perm[:, O0 + 512 : O0 + 1024]).astype(BF16)
        vp[:, 1024:1280] = dot(vb[...], perm[:, HI0 : HI0 + KREM]).astype(BF16)

    def work_attend(h):
        same = (
            lax.rem(lax.broadcasted_iota(jnp.int32, (128, 128), 0), 8)
            == lax.rem(lax.broadcasted_iota(jnp.int32, (128, 128), 1), 8)
        ).astype(F32)
        rows = pl.ds(h * 128, 128)
        num_rem = den_rem = None
        for g in range(4):
            probs = []
            for a in range(4):
                hd = 4 * g + a
                w = (HD * hd) // 128 * 128
                width = min(256, D - w)
                lane = lax.broadcasted_iota(jnp.int32, (16, width), 1) + w
                pick = jnp.logical_and(lane >= HD * hd, lane < HD * (hd + 1)).astype(F32).astype(BF16)
                pick = jnp.concatenate([pick] * 8, axis=0)
                kw = qk[1, rows, w : w + width] * pick
                sc = lax.dot_general(qk[0, rows, w : w + width], kw, (((1,), (1,)), ((), ())), preferred_element_type=F32)
                probs.append((jnp.exp2(sc) * same).astype(BF16))
            p4 = jnp.concatenate(probs, axis=1)
            vg = jnp.concatenate([
                vp[rows, g * 128 : g * 128 + 128],
                vp[rows, 512 + g * 128 : 512 + g * 128 + 128],
                vp[rows, 1024 + (g // 2) * 128 : 1024 + (g // 2) * 128 + 128],
            ], axis=1)
            mk = masks[g % 2]
            num = dot(p4, jnp.concatenate([vg] * 4, axis=0) * mk)
            den = dot(p4, mk)
            inv = 1.0 / den[:, 0:128]
            attp[rows, g * 128 : g * 128 + 128] = (num[:, 0:128] * inv).astype(BF16)
            attp[rows, 512 + g * 128 : 512 + g * 128 + 128] = (num[:, 128:256] * inv).astype(BF16)
            if g % 2 == 0:
                num_rem, den_rem = num[:, 256:384], den[:, 256:384]
            else:
                lo = 1024 + (g // 2) * 128
                attp[rows, lo : lo + 128] = ((num_rem + num[:, 256:384]) / (den_rem + den[:, 256:384])).astype(BF16)

    work = {
        "tab": work_tab,
        "mod": work_mod,
        "rope": work_rope,
        "ln": work_ln,
        "p0": lambda: work_permute(0),
        "p1": lambda: work_permute(1),
        "p2": lambda: work_permute(2),
        "f0": lambda: work_multiply(par, "E"),
        "f1": work_stats,
        "f2": lambda: work_turn(par),
        "g0": lambda: work_multiply(1 - par, "YE"),
        "g1": work_stats,
        "g2": lambda: work_turn(1 - par),
        "v": work_values,
        "vp": work_permute_values,
        "a0": lambda: work_attend(0),
        "a1": lambda: work_attend(1),
    }

    send_onehots()
    for name, hop, *more in SCHEDULE:
        if name in work:
            work[name]()
        elif name not in KINDS:
            send_hidden(name)
        elif hop < 0:
            start_own(name)
        else:
            take(name, hop, more[0] if more else 0)

    from_sibling(("C", "YC"))

    def o_rows(cc):
        return lambda cols: jnp.concatenate([oc[0, cc, :, :, cols], oc[1, cc, :, :, cols]], axis=1).reshape(512, NT)

    project(delta, lambda: attp[...], [o_rows(0), o_rows(1), piece(par, 1, 32)])

    for place in far_first:
        to_frame = partner(*place)
        f = lax.rem(to_frame + NF - 1, NF)
        r16 = pl.ds(pl.multiple_of(f * TOK, TOK), TOK)
        r8 = pl.multiple_of(f * 8, 8)
        gate = modul[2, pl.ds(r8, 8), :]
        both = jnp.concatenate([
            gate * delta[pl.ds(r8, 8), :],
            gate * delta[pl.ds(pl.multiple_of(r8 + 128, 8), 8), :],
        ], axis=0)
        upd[r16, :] = (x_v[r16, :].astype(F32) + both).astype(BF16)
        to_band = band + f // (NF - 1)
        goes = to_band < NB
        if place == (0, 0):
            goes = jnp.logical_and(goes, frame == 0)
            stay = pltpu.make_async_copy(upd.at[r16], out.at[own], local.at[0])

            @pl.when(frame > 0)
            def _():
                stay.start()
                stay.wait()

        pl.when(goes)(functools.partial(push, upd.at[r16], out.at[own], (to_band, to_frame), 14, FIN))

    some, most = pl.ds(0, ROWS - 2 * TOK), pl.ds(0, ROWS - TOK)
    starts, ends = frame == 0, band == NB - 1
    both_ways = jnp.logical_and
    pl.when(both_ways(starts, band > 0))(lambda: settle(out, rsem=FIN))
    pl.when(frame > 0)(lambda: settle(out.at[most], rsem=FIN))
    pl.when(both_ways(starts, band < NB - 1))(lambda: settle(upd, ssem=14))
    pl.when(starts == ends)(lambda: settle(upd.at[most], ssem=14))
    pl.when(both_ways(frame > 0, ends))(lambda: settle(upd.at[some], ssem=14))
    settle(hidden.at[most], ssem=12)
    settle(onehot.at[pl.ds(0, NF - 1)], ssem=13)
    for n, kind in enumerate(KINDS):
        settle(same_bytes(NF - 1, kind), ssem=n)
        settle(same_bytes(NF - 1, kind), ssem=6 + n)


def local_step(hidden, timesteps, ada_table, w_qkv, w_out, q_gain, k_gain, fresh):
    hbm = pl.BlockSpec(memory_space=pl.ANY)
    consts = constants()
    shapes = [
        pltpu.VMEM((2, 2, 16, 64, D), BF16),
        pltpu.VMEM((2, 2, 16, 16, D), BF16),
        pltpu.VMEM((72, 3 * D), BF16),
        pltpu.VMEM((72, D), BF16),
        pltpu.VMEM((ROWS, D), BF16),
        pltpu.VMEM((3, STEPS, D), F32),
        pltpu.VMEM((3, 128, D), F32),
        pltpu.VMEM((NF, 8, 128), F32),
        *[pltpu.VMEM(a.shape, a.dtype) for a in consts],
        pltpu.VMEM((2, 1, HD), F32),
        pltpu.VMEM((3, 128, D), F32),
        pltpu.VMEM((2, 3, 128, D), F32),
        pltpu.VMEM((ROWS, D), F32),
        pltpu.VMEM((ROWS, D), BF16),
        pltpu.VMEM((ROWS, O0), BF16),
        pltpu.VMEM((ROWS, D), F32),
        pltpu.VMEM((ROWS, D), F32),
        pltpu.VMEM((2, ROWS, D), BF16),
        pltpu.VMEM((ROWS, D), BF16),
        pltpu.VMEM((ROWS, 1280), BF16),
        pltpu.VMEM((ROWS, 1280), BF16),
        pltpu.VMEM((ROWS, D), F32),
        pltpu.VMEM((ROWS, D), BF16),
        pltpu.SemaphoreType.DMA((15,)),
        pltpu.SemaphoreType.DMA((45,)),
        pltpu.SemaphoreType.DMA((12,)),
    ]
    moved = pl.pallas_call(
        kernel,
        out_shape=jax.ShapeDtypeStruct((ROWS, D), BF16),
        in_specs=[hbm, pl.BlockSpec(memory_space=pltpu.SMEM)] + [hbm] * (5 + len(consts)),
        out_specs=hbm,
        scratch_shapes=shapes,
        compiler_params=pltpu.CompilerParams(collective_id=0, has_side_effects=True, vmem_limit_bytes=56 << 20),
        name="queue_step",
    )(hidden[0, 0], timesteps, jnp.transpose(ada_table, (1, 0, 2)), w_qkv, w_out, q_gain[None], k_gain[None], *consts)
    first = jnp.logical_and(lax.axis_index("band") == 0, lax.axis_index("frame") == 0)
    return jnp.where(first, fresh, moved)[None, None]


def solution(mesh):
    return jax.shard_map(
        local_step,
        mesh=mesh,
        in_specs=(
            P("band", "frame", None, None),
            P("band", "frame"),
            P(),
            P("frame", None),
            P("frame", None),
            P(),
            P(),
            P(),
        ),
        out_specs=P("band", "frame", None, None),
        check_vma=False,
    )
```
